512 devices in a mesh: island: 16 (over z_hi, y), fsdp: 32 (over z_lo, x, core).
Axes of the slice: x: 4, y: 8, z: 8 (z_hi: 2, z_lo: 4; z = z_hi * 4 + z_lo), core: 2. Of those that a mesh axis runs over, the one named last changes fastest.
Arguments:
- activations: bfloat16 [98304, 8192], P(('island', 'fsdp')), may hold values from -6 to 6
- local_weights: bfloat16 [16, 8192, 512], P('island', 'fsdp'), may hold values from -0.0625 to 0.0625
- grad_codes: int32 [16, 8192, 512], P('island', 'fsdp'), may hold values from -8 to 7
- block_scales: float32 [16, 8192, 4], P('island', 'fsdp'), may hold values from 0.03 to 0.5
- global_weights: bfloat16 [8192, 512], P('fsdp'), may hold values from -3 to 3
- momentum: bfloat16 [16, 8192, 512], P('island', 'fsdp'), may hold values from -3 to 3
- block_owner: int32 [8192, 4], P('fsdp'), may hold values from 0 to 15
Outputs:
- projected_keys: bfloat16 [98304, 512], P(('island', 'fsdp'))
- new_global: bfloat16 [8192, 512], P('fsdp')
- new_momentum: bfloat16 [8192, 512], P('fsdp')
The draws below stay inside these ranges and needn't reach their ends.
Inputs may be any that keep to these rules, and one draw needn't show every extreme that they name: `grad_codes`: codes of a signed 4-bit quantizer.
All inputs are finite; a program needn't handle non-finite values.
Results may differ from the reference program's by a relative error of at most 0.001.
Values may be sent and summed in bfloat16 or wider, within the bound.
A program may use at most 64 MiB of HBM per device.

```python
import math
import jax
import jax.numpy as jnp
from jax import lax

D = 8192
KVW = 512
BLOCK = 128
TOK_DEV = 192
TOKENS = 98304
N_ISLAND = 16
N_FSDP = 32


def plant(drawn, own_key, least, high):
    extent = drawn.shape
    place = [jax.random.randint(jax.random.fold_in(own_key, axis), (), 0, extent[axis]) for axis in range(len(extent))]
    drawn = drawn.at[tuple(place)].set(least)
    longest = extent.index(max(extent))
    place[longest] = (place[longest] + 1) % extent[longest]
    return drawn.at[tuple(place)].set(high)


def block_levels(key, extent, pieces, low, high):
    gain = 1.0
    for position, blocks in pieces:
        heights = jax.random.uniform(jax.random.fold_in(jax.random.fold_in(key, 6), position), (blocks,), jnp.float32, low / len(pieces), high / len(pieces))
        gain = gain * jnp.repeat(jnp.exp(heights), extent[position] // blocks).reshape((-1,) + (1,) * (len(extent) - 1 - position))
    return gain


def gaussian(stream_key, extent, width, reach, cuts=(), held_as=jnp.bfloat16):
    values = jax.random.normal(stream_key, extent, jnp.float32) * width
    if len(cuts) > 0:
        values = block_levels(stream_key, extent, cuts, -0.22, 0.18) * values
    return jnp.clip(values, min=-reach, max=reach).astype(held_as)


def setup_inputs(seed: int = 0) -> dict:
    key_of = jax.random.split(jax.random.key(seed), 8)
    activations = gaussian(key_of[0], (TOKENS, D), 1.0, 6.0, ((0, 512),))
    local_weights = gaussian(key_of[1], (N_ISLAND, D, KVW), D ** -0.5, 0.0625, ((0, 16), (1, 32)))
    grad_codes = plant(jax.random.randint(key_of[2], (N_ISLAND, D, KVW), -8, 8), jax.random.fold_in(key_of[2], 1), -8, 7).astype(jnp.int32)
    block_scales = jnp.clip(jnp.exp(math.log(0.5) - 2.8134107 * jax.random.uniform(key_of[3], (N_ISLAND, D, KVW // BLOCK), jnp.float32) ** block_levels(key_of[3], (N_ISLAND, D, KVW // BLOCK), ((0, 16), (1, 32)), -0.2, 0.2)), 0.03, 0.5)
    global_weights = gaussian(key_of[4], (D, KVW), 0.5, 3.0, ((0, 32),))
    momentum = gaussian(key_of[5], (N_ISLAND, D, KVW), 0.5, 3.0, ((0, 16), (1, 32)))
    block_owner = plant(jax.random.randint(key_of[6], (D, KVW // BLOCK), 0, N_ISLAND), jax.random.fold_in(key_of[6], 1), 0, N_ISLAND - 1).astype(jnp.int32)
    return dict(activations=activations, local_weights=local_weights, grad_codes=grad_codes, block_scales=block_scales, global_weights=global_weights, momentum=momentum, block_owner=block_owner)


outer_momentum = 0.9
outer_rate = 0.7


def reference(activations, local_weights, grad_codes, block_scales, global_weights, momentum, block_owner):
    island_rows = activations.reshape(N_ISLAND, N_FSDP * TOK_DEV, D)

    def project(paired):
        token_block, weights = paired
        return jnp.dot(token_block, weights, preferred_element_type=jnp.float32).astype(jnp.bfloat16)

    projected = lax.map(project, (island_rows, local_weights)).reshape(N_ISLAND * N_FSDP * TOK_DEV, KVW)
    block_count = KVW // BLOCK
    pseudo = grad_codes.reshape(N_ISLAND, D, block_count, BLOCK).astype(jnp.float32) * block_scales[..., None]
    mean_delta = jnp.sum(pseudo, axis=0) / N_ISLAND
    islands = jnp.arange(N_ISLAND, dtype=jnp.int32)
    chosen = (block_owner[None] == islands[:, None, None])[..., None]
    stored = momentum.reshape(N_ISLAND, D, block_count, BLOCK).astype(jnp.float32)
    owned_state = jnp.sum(jnp.where(chosen, stored, jnp.zeros_like(stored)), axis=0)
    fresh = outer_momentum * owned_state + mean_delta
    new_momentum = fresh.astype(jnp.bfloat16).reshape(D, KVW)
    global_f32 = global_weights.reshape(D, block_count, BLOCK).astype(jnp.float32)
    new_global = (global_f32 - outer_rate * (mean_delta + outer_momentum * fresh)).astype(jnp.bfloat16).reshape(D, KVW)
    return projected, new_global, new_momentum
```

```python
import functools

import jax
import jax.numpy as jnp
from jax import lax
from jax.experimental import pallas as pl
from jax.experimental.pallas import tpu as pltpu
from jax.sharding import PartitionSpec as P

MESH = pl.DeviceIdType.MESH

outer_momentum = 0.9
outer_rate = 0.7

NX, NZ, NY = 4, 4, 8
Q = 32


def gather_kernel(
    act, wown, codes, scales, owner, gw, mom,
    proj, og, om,
    X, W, acc, pacc,
    cbuf, stg, rbuf, scbuf, rsc, owbuf, gbuf, tmp, tmpt, zs, zm, zrs, zrm, res,
    lsem, zsem_s, zsem_r, xsem_s, xsem_r, qxs, qxr, qzs, qzr,
    acts, actr, pts, ptr_, rss, rsr, scs, scr, zhs, zhr, ags, agr, osem,
):
    i, f = lax.axis_index("island"), lax.axis_index("fsdp")
    zh, y = i // NY, i % NY
    z, x, c = f // (2 * NX), (f // 2) % NX, f % 2
    rows = wown.shape[0]
    p = rows - Q
    hp = p // 2
    tok = act.shape[0]
    depth = rows

    def fs(zz, xx, cc):
        return {"fsdp": zz * 2 * NX + xx * 2 + cc}

    def isl(hh, yy):
        return {"island": hh * NY + yy}

    xl, xr, xo = (x + NX - 1) % NX, (x + 1) % NX, (x + 2) % NX
    right, left = fs(z, xr, c), fs(z, xl, c)
    partner = fs(z, x, 1 - c)
    far = isl(1 - zh, y)

    def rcopy(src, dst, ss, rs, dev):
        return pltpu.make_async_remote_copy(
            src_ref=src, dst_ref=dst, send_sem=ss, recv_sem=rs, device_id=dev, device_id_type=MESH
        )

    kown = z * NX + x
    ld_codes = pltpu.make_async_copy(codes, cbuf, lsem.at[0])
    ld_codes.start()
    ld_w = pltpu.make_async_copy(wown, W.at[kown], lsem.at[1])
    ld_w.start()
    ld_mom = pltpu.make_async_copy(mom, stg.at[:, :, pl.ds(16, 16), :], lsem.at[2])
    ld_mom.start()
    ld_sc = pltpu.make_async_copy(scales, scbuf, lsem.at[3])
    ld_sc.start()
    ld_ow = pltpu.make_async_copy(owner, owbuf, lsem.at[4])
    ld_ow.start()
    ld_gw = pltpu.make_async_copy(gw.at[y], gbuf, lsem.at[5])
    ld_gw.start()

    @pl.loop(0, NX * NZ)
    def _(k):
        col = pl.multiple_of((2 * k + c) * depth, depth)
        pltpu.make_async_copy(
            act.at[:, pl.ds(col, depth)], X.at[k, pl.ds(0, tok), :], lsem.at[6]
        ).start()

    bar = pltpu.get_barrier_semaphore()
    zg = zh * NZ + z
    zup, zdn = (zg + 1) % (2 * NZ), (zg + 2 * NZ - 1) % (2 * NZ)
    peers = [right, left, partner, far]
    peers += [isl(zh, (y + d) % NY) for d in range(1, NY)]
    peers += [
        {"island": (n // NZ) * NY + y, "fsdp": (n % NZ) * 2 * NX + x * 2 + c} for n in (zup, zdn)
    ]
    for dev in peers:
        pl.semaphore_signal(bar, inc=1, device_id=dev, device_id_type=MESH)

    ld_codes.wait()

    @pl.loop(0, NY)
    def _(t):
        stg[t, :, pl.ds(0, 16), :] = cbuf[t].astype(jnp.float32).astype(jnp.bfloat16)

    ld_w.wait()
    ld_mom.wait()
    ld_sc.wait()
    pl.semaphore_wait(bar, len(peers))

    def half(k, h):
        return W.at[k, pl.ds(h * hp, hp), :]

    def qpart(k):
        return W.at[k, pl.ds(p, Q), :]

    def qhalf(k, h):
        return W.at[k, pl.ds(p + h * (Q // 2), Q // 2), :]

    def qrow(r):
        return W.at[pl.ds(r * NX, NX), pl.ds(p, Q), :]

    m = z // 2
    e = z * (1 - m) + (NZ - 1 - z) * m

    def order(j):
        g = j if j >= 2 else j * (1 - e) + (1 - j) * e
        return g * (1 - m) + (NZ - 1 - g) * m

    def xcopy(j, n):
        r = order(j) * NX
        k, h, dev = [
            (r + x, 0, right), (r + x, 1, right), (r + x, 1, left), (r + x, 0, left),
            (r + xl, 0, right), (r + xr, 1, left),
        ][n]
        return rcopy(half(k, h), half(k, h), xsem_s.at[j, n], xsem_r.at[j, n], dev)

    def xlanded(j, n):
        r = order(j) * NX
        k, h = [(r + xl, 0), (r + xl, 1), (r + xr, 1), (r + xr, 0), (r + xo, 0), (r + xo, 1)][n]
        return rcopy(half(k, h), half(k, h), xsem_s.at[j, n], xsem_r.at[j, n], right)

    def qxcopy(n):
        k = [kown, kown, z * NX + xl, z * NX + xr][n]
        dev = [right, left, right, left][n]
        ref = qpart(k) if n < 2 else qhalf(k, n - 2)
        return rcopy(ref, ref, qxs.at[n], qxr.at[n], dev)

    def qxlanded(n):
        k = z * NX + [xl, xr, xo, xo][n]
        ref = qpart(k) if n < 2 else qhalf(k, n - 2)
        return rcopy(ref, ref, qxs.at[n], qxr.at[n], right)

    up, down = fs(z + 1, x, c), fs(z - 1, x, c)

    def zcopy(s, h, d):
        k = (z - s if d == 0 else z + s) * NX + x
        return rcopy(half(k, h), half(k, h), zsem_s.at[s, h, d], zsem_r.at[s, h, d], up if d == 0 else down)

    def zlanded(s, h, d):
        k = (z - s if d == 0 else z + s) * NX + x
        return rcopy(half(k, h), half(k, h), zsem_s.at[s - 1, h, d], zsem_r.at[s - 1, h, d], up if d == 0 else down)

    def qzcopy(s, d):
        ref = qrow(z - s if d == 0 else z + s)
        return rcopy(ref, ref, qzs.at[s, d], qzr.at[s, d], up if d == 0 else down)

    def qzlanded(s, d):
        ref = qrow(z - s if d == 0 else z + s)
        return rcopy(ref, ref, qzs.at[s - 1, d], qzr.at[s - 1, d], up if d == 0 else down)

    def has(s, d):
        return z - s >= 0 if d == 0 else z + s <= NZ - 1

    def goes(d):
        return z < NZ - 1 if d == 0 else z > 0

    def zpass(s):
        for h in range(2):
            for d in range(2):
                @pl.when(has(s, d))
                def _():
                    zlanded(s, h, d).wait_recv()

                    @pl.when(goes(d))
                    def _():
                        zcopy(s, h, d).start()

    def qzpass(s):
        for d in range(2):
            @pl.when(has(s, d))
            def _():
                qzlanded(s, d).wait_recv()

                @pl.when(goes(d))
                def _():
                    qzcopy(s, d).start()

    def xsend(j):
        for n in (0, 2, 1, 3):
            xcopy(j, n).start()

    def xpass(j):
        for n in (0, 2):
            xlanded(j, n).wait_recv()
            xcopy(j, 4 + n // 2).start()

    def xdone(j):
        for n in (1, 3, 4, 5):
            xlanded(j, n).wait_recv()

    def multiply(k, first=False):
        part = jnp.dot(X[k], W[k], preferred_element_type=jnp.float32)
        if first:
            acc[...] = part
        else:
            acc[...] += part

    def multiply_row(j):
        r = order(j) * NX

        @pl.loop(0, NX)
        def _(n):
            multiply(r + n)

    def rs_copy(hf, d):
        t = (y + d) % NY
        return rcopy(stg.at[t, hf], rbuf.at[hf, d - 1], rss.at[hf], rsr.at[hf], isl(zh, t))

    def sc_copy(d):
        t = (y + d) % NY
        lanes = pl.ds(pl.multiple_of((t // 4) * 128, 128), 128)
        return rcopy(scbuf.at[:, lanes], rsc.at[d - 1], scs, scr, isl(zh, t))

    def zh_copies(hf):
        return (
            rcopy(zs.at[hf], zrs.at[hf], zhs.at[hf, 0], zhr.at[hf, 0], far),
            rcopy(zm.at[hf], zrm.at[hf], zhs.at[hf, 1], zhr.at[hf, 1], far),
        )

    def ag_copy(hf, d):
        return rcopy(res.at[hf, y], res.at[hf, y], ags.at[hf], agr.at[hf], isl(zh, (y + d) % NY))

    far_first = (4, 3, 5, 2, 6, 1, 7)

    def small_columns():
        rcopy(rsc, rsc, scs, scr, far).wait_recv()
        ld_ow.wait()
        lanes = pl.ds(pl.multiple_of((y // 4) * 128, 128), 128)
        tmp[...] = jnp.zeros_like(tmp)
        tmp[pl.ds(0, 4), :] = scbuf[:, lanes]
        for d in range(1, NY):
            tmp[pl.ds(4 * d, 4), :] = rsc[d - 1]
        tmp[pl.ds(32, 4), :] = owbuf[:, lanes].astype(jnp.float32)
        tmpt[...] = tmp[...].T

    def partial(hf):
        rcopy(rbuf.at[hf], rbuf.at[hf], rss.at[hf], rsr.at[hf], far).wait_recv()
        cols = tmpt[pl.ds(pl.multiple_of(32 * (y % 4) + 16 * hf, 16), 16), :]
        for b in range(4):
            lanes = pl.ds(128 * b, 128)
            total = jnp.zeros((16, 128), jnp.float32)
            held = jnp.zeros((16, 128), jnp.float32)
            own = jnp.broadcast_to(cols[:, 32 + b : 33 + b], (16, 128))
            for d in range(NY):
                if d == 0:
                    code, state = stg[y, hf, pl.ds(0, 16), lanes], stg[y, hf, pl.ds(16, 16), lanes]
                else:
                    code, state = (
                        rbuf[hf, d - 1, pl.ds(0, 16), lanes],
                        rbuf[hf, d - 1, pl.ds(16, 16), lanes],
                    )
                total += code.astype(jnp.float32) * cols[:, 4 * d + b : 4 * d + b + 1]
                who = (zh * NY + (y + NY - d) % NY).astype(jnp.float32)
                held += jnp.where(own == who, state.astype(jnp.float32), 0.0)
            zs[hf, :, lanes] = total
            zm[hf, :, lanes] = held.astype(jnp.bfloat16)
        for cp in zh_copies(hf):
            cp.start()

    def finish(hf):
        for cp in zh_copies(hf):
            cp.wait_recv()
        mean = (zs[hf] + zrs[hf]) * (1.0 / (2 * NY))
        held = zm[hf].astype(jnp.float32) + zrm[hf].astype(jnp.float32)
        fresh = outer_momentum * held + mean
        updated = gbuf[hf].astype(jnp.float32) - outer_rate * (mean + outer_momentum * fresh)
        res[hf, y, 0] = updated.astype(jnp.bfloat16)
        res[hf, y, 1] = fresh.astype(jnp.bfloat16)
        for d in far_first:
            ag_copy(hf, d).start()

    qxcopy(0).start()
    qxcopy(1).start()
    xsend(0)
    for h in range(2):
        for d in range(2):
            @pl.when(goes(d))
            def _():
                zcopy(0, h, d).start()
    for hf in range(2):
        for d in far_first:
            rs_copy(hf, d).start()
        if hf == 0:
            for d in far_first:
                sc_copy(d).start()

    @pl.loop(0, NX * NZ)
    def _(k):
        col = pl.multiple_of((2 * k + 1 - c) * depth, depth)
        rcopy(act.at[:, pl.ds(col, depth)], X.at[k, pl.ds(tok, tok), :], acts, actr, partner).start()

    for n in range(2):
        qxlanded(n).wait_recv()
        qxcopy(2 + n).start()
    zpass(1)
    xsend(1)
    xpass(0)
    for n in (2, 3):
        qxlanded(n).wait_recv()
    for d in range(2):
        @pl.when(goes(d))
        def _():
            qzcopy(0, d).start()
    small_columns()
    partial(0)
    zpass(2)
    xsend(2)
    xpass(1)
    xdone(0)
    rcopy(X.at[:, pl.ds(tok, tok), :], X.at[:, pl.ds(tok, tok), :], acts, actr, partner).wait_recv()
    pltpu.make_async_copy(X.at[:, pl.ds(0, tok), :], X.at[:, pl.ds(0, tok), :], lsem.at[6]).wait()
    acc[...] = jnp.zeros_like(acc)
    partial(1)
    zpass(3)
    xsend(3)
    multiply_row(0)
    qzpass(1)
    xpass(2)
    ld_gw.wait()
    finish(0)
    qzpass(2)
    xdone(1)
    qzpass(3)
    multiply_row(1)
    xpass(3)
    finish(1)
    xdone(2)
    multiply_row(2)
    xdone(3)
    multiply_row(3)

    pcopy = rcopy(acc.at[pl.ds(tok, tok), :], pacc, pts, ptr_, partner)
    pcopy.start()
    for hf in range(2):
        rcopy(res.at[hf, pl.ds(0, 7)], res.at[hf, pl.ds(0, 7)], ags.at[hf], agr.at[hf], far).wait_recv()
    outs = []
    for hf in range(2):
        for n, out in enumerate((og, om)):
            cp = pltpu.make_async_copy(res.at[hf, :, n], out.at[:, hf], osem.at[hf, n])
            cp.start()
            outs.append(cp)
    pcopy.wait_recv()
    proj[...] = (acc[pl.ds(0, tok), :] + pacc[...]).astype(jnp.bfloat16)

    for j in range(NZ):
        for n in range(6):
            xcopy(j, n).wait_send()
    for n in range(4):
        qxcopy(n).wait_send()
    for s in range(NZ):
        for d in range(2):
            if s < NZ - 1:
                @pl.when(has(s, d) & goes(d))
                def _():
                    for h in range(2):
                        zcopy(s, h, d).wait_send()
                    qzcopy(s, d).wait_send()
    rcopy(X.at[:, pl.ds(tok, tok), :], X.at[:, pl.ds(tok, tok), :], acts, actr, partner).wait_send()
    rcopy(rsc, rsc, scs, scr, far).wait_send()
    for hf in range(2):
        rcopy(rbuf.at[hf], rbuf.at[hf], rss.at[hf], rsr.at[hf], far).wait_send()
        for cp in zh_copies(hf):
            cp.wait_send()
        rcopy(res.at[hf, pl.ds(0, 7)], res.at[hf, pl.ds(0, 7)], ags.at[hf], agr.at[hf], far).wait_send()
    pcopy.wait_send()
    for cp in outs:
        cp.wait()


def body(
    activations, local_weights, grad_codes, block_scales, global_weights, momentum, block_owner
):
    tok, model = activations.shape
    rows, width = local_weights.shape[1:]
    nk = NX * NZ
    cut = (NY, 2, rows // (2 * NY), width)
    any_space = pl.BlockSpec(memory_space=pl.ANY)
    vmem = pl.BlockSpec(memory_space=pltpu.VMEM)
    bf, f32 = jnp.bfloat16, jnp.float32
    dma = pltpu.SemaphoreType.DMA
    proj, og, om = pl.pallas_call(
        gather_kernel,
        out_shape=(
            jax.ShapeDtypeStruct((tok, width), bf),
            jax.ShapeDtypeStruct(cut, bf),
            jax.ShapeDtypeStruct(cut, bf),
        ),
        in_specs=[any_space] * 7,
        out_specs=(vmem, any_space, any_space),
        scratch_shapes=[
            pltpu.VMEM((nk, 2 * tok, rows), bf),
            pltpu.VMEM((nk, rows, width), bf),
            pltpu.VMEM((2 * tok, width), f32),
            pltpu.VMEM((tok, width), f32),
            pltpu.VMEM(cut, jnp.int32),
            pltpu.VMEM((NY, 2, 32, width), bf),
            pltpu.VMEM((2, NY - 1, 32, width), bf),
            pltpu.VMEM((4, rows), f32),
            pltpu.VMEM((NY - 1, 4, 128), f32),
            pltpu.VMEM((4, rows), jnp.int32),
            pltpu.VMEM((2, 16, width), bf),
            pltpu.VMEM((128, 128), f32),
            pltpu.VMEM((128, 128), f32),
            pltpu.VMEM((2, 16, width), f32),
            pltpu.VMEM((2, 16, width), bf),
            pltpu.VMEM((2, 16, width), f32),
            pltpu.VMEM((2, 16, width), bf),
            pltpu.VMEM((2, NY, 2, 16, width), bf),
            dma((7,)),
            dma((NZ, 2, 2)), dma((NZ, 2, 2)),
            dma((NZ, 6)), dma((NZ, 6)),
            dma((4,)), dma((4,)),
            dma((NZ, 2)), dma((NZ, 2)),
            dma, dma,
            dma, dma,
            dma((2,)), dma((2,)),
            dma, dma,
            dma((2, 2)), dma((2, 2)),
            dma((2,)), dma((2,)),
            dma((2, 2)),
        ],
        compiler_params=pltpu.CompilerParams(
            collective_id=0, has_side_effects=True, vmem_limit_bytes=40 * 2**20
        ),
        name="sync_and_project",
    )(
        activations,
        local_weights[0],
        grad_codes[0].reshape(cut),
        block_scales[0].T,
        block_owner.T,
        global_weights.reshape(cut),
        momentum[0].reshape(cut),
    )
    return proj, og.reshape(rows, width), om.reshape(rows, width)


def solution(mesh):
    return jax.shard_map(
        body,
        mesh=mesh,
        in_specs=(
            P(("island", "fsdp"), None),
            P("island", "fsdp", None),
            P("island", "fsdp", None),
            P("island", "fsdp", None),
            P("fsdp", None),
            P("island", "fsdp", None),
            P("fsdp", None),
        ),
        out_specs=(P(("island", "fsdp"), None), P("fsdp", None), P("fsdp", None)),
        check_vma=False,
    )
```

```python
import functools

import jax
import jax.numpy as jnp
from jax import lax
from jax.experimental import pallas as pl
from jax.experimental.pallas import tpu as pltpu
from jax.sharding import PartitionSpec as P

MESH = pl.DeviceIdType.MESH

outer_momentum = 0.9
outer_rate = 0.7

NX, NZ, NY = 4, 4, 8
Q = 32


def gather_kernel(
    act, wown, codes, scales, owner, gw, mom,
    proj, og, om,
    X, W, acc, pacc,
    cbuf, stg, rbuf, scbuf, rsc, owbuf, gbuf, tmp, tmpt, zs, zm, zrs, zrm, res,
    lsem, zsem_s, zsem_r, xsem_s, xsem_r, qxs, qxr, qzs, qzr,
    acts, actr, pts, ptr_, rss, rsr, scs, scr, zhs, zhr, ags, agr, osem, farsem, heresem,
):
    i, f = lax.axis_index("island"), lax.axis_index("fsdp")
    zh, y = i // NY, i % NY
    z, x, c = f // (2 * NX), (f // 2) % NX, f % 2
    rows = wown.shape[0]
    p = rows - Q
    hp = p // 2
    tok = act.shape[0]
    depth = rows

    def fs(zz, xx, cc):
        return {"fsdp": zz * 2 * NX + xx * 2 + cc}

    def isl(hh, yy):
        return {"island": hh * NY + yy}

    xl, xr, xo = (x + NX - 1) % NX, (x + 1) % NX, (x + 2) % NX
    right, left = fs(z, xr, c), fs(z, xl, c)
    partner = fs(z, x, 1 - c)
    far = isl(1 - zh, y)

    def rcopy(src, dst, ss, rs, dev):
        return pltpu.make_async_remote_copy(
            src_ref=src, dst_ref=dst, send_sem=ss, recv_sem=rs, device_id=dev, device_id_type=MESH
        )

    g = y // 5
    rank = (1 - g) * (2 * y - 1 + (NY - y) // NY) + g * 2 * (NY - y)

    def rank_of(t):
        gt = t // 5
        return (1 - gt) * (2 * t - 1 + (NY - t) // NY) + gt * 2 * (NY - t)

    up, down = fs(z + 1, x, c), fs(z - 1, x, c)
    bar = pltpu.get_barrier_semaphore()

    def hello(dev):
        pl.semaphore_signal(bar, inc=1, device_id=dev, device_id_type=MESH)

    ld_w = pltpu.make_async_copy(wown, W.at[z * NX + x], lsem.at[1])
    ld_w.start()
    for dev in (right, left, partner):
        hello(dev)

    @pl.when(z < NZ - 1)
    def _():
        hello(up)

    @pl.when(z > 0)
    def _():
        hello(down)

    for d in range(1, NY):
        t = (y + d) % NY

        @pl.when(rank_of(t) > rank)
        def _():
            hello(isl(zh, t))

    @pl.when(zh == 0)
    def _():
        hello(far)

    kown = z * NX + x
    ld_codes = pltpu.make_async_copy(codes, cbuf, lsem.at[0])
    ld_codes.start()
    ld_mom = pltpu.make_async_copy(mom, stg.at[:, :, pl.ds(16, 16), :], lsem.at[2])
    ld_mom.start()
    ld_sc = pltpu.make_async_copy(scales, scbuf, lsem.at[3])
    ld_sc.start()
    ld_ow = pltpu.make_async_copy(owner, owbuf, lsem.at[4])
    ld_ow.start()
    ld_gw = pltpu.make_async_copy(gw.at[y], gbuf, lsem.at[5])
    ld_gw.start()

    edge = 1 - (z + 1) // NZ + (z + NZ - 1) // NZ
    ld_w.wait()
    pl.semaphore_wait(bar, 3 + edge + rank + zh)

    def answer():
        for d in range(1, NY):
            t = (y + d) % NY

            @pl.when(rank_of(t) < rank)
            def _():
                pl.semaphore_signal(heresem, inc=1, device_id=isl(zh, t), device_id_type=MESH)

        @pl.when(zh == 1)
        def _():
            pl.semaphore_signal(farsem, inc=1, device_id=far, device_id_type=MESH)

    def x_start():
        @pl.loop(0, NX * NZ)
        def _(k):
            col = pl.multiple_of((2 * k + c) * depth, depth)
            pltpu.make_async_copy(
                act.at[:, pl.ds(col, depth)], X.at[k, pl.ds(0, tok), :], lsem.at[6]
            ).start()

    def codes_ready():
        ld_codes.wait()

        @pl.loop(0, NY)
        def _(t):
            stg[t, :, pl.ds(0, 16), :] = cbuf[t].astype(jnp.float32).astype(jnp.bfloat16)

        ld_mom.wait()
        ld_sc.wait()

    def peers_here():
        @pl.when(rank < NY - 1)
        def _():
            pl.semaphore_wait(heresem, NY - 1 - rank)

    def half(k, h):
        return W.at[k, pl.ds(h * hp, hp), :]

    def qpart(k):
        return W.at[k, pl.ds(p, Q), :]

    def qhalf(k, h):
        return W.at[k, pl.ds(p + h * (Q // 2), Q // 2), :]

    def qrow(r):
        return W.at[pl.ds(r * NX, NX), pl.ds(p, Q), :]

    m = z // 2
    e = z * (1 - m) + (NZ - 1 - z) * m

    def order(j):
        g = j if j >= 2 else j * (1 - e) + (1 - j) * e
        return g * (1 - m) + (NZ - 1 - g) * m

    def xcopy(j, n):
        r = order(j) * NX
        k, h, dev = [
            (r + x, 0, right), (r + x, 1, right), (r + x, 1, left), (r + x, 0, left),
            (r + xl, 0, right), (r + xr, 1, left),
        ][n]
        return rcopy(half(k, h), half(k, h), xsem_s.at[j, n], xsem_r.at[j, n], dev)

    def xlanded(j, n):
        r = order(j) * NX
        k, h = [(r + xl, 0), (r + xl, 1), (r + xr, 1), (r + xr, 0), (r + xo, 0), (r + xo, 1)][n]
        return rcopy(half(k, h), half(k, h), xsem_s.at[j, n], xsem_r.at[j, n], right)

    def qxcopy(n):
        k = [kown, kown, z * NX + xl, z * NX + xr][n]
        dev = [right, left, right, left][n]
        ref = qpart(k) if n < 2 else qhalf(k, n - 2)
        return rcopy(ref, ref, qxs.at[n], qxr.at[n], dev)

    def qxlanded(n):
        k = z * NX + [xl, xr, xo, xo][n]
        ref = qpart(k) if n < 2 else qhalf(k, n - 2)
        return rcopy(ref, ref, qxs.at[n], qxr.at[n], right)

    def zcopy(s, h, d):
        k = (z - s if d == 0 else z + s) * NX + x
        return rcopy(half(k, h), half(k, h), zsem_s.at[s, h, d], zsem_r.at[s, h, d], up if d == 0 else down)

    def zlanded(s, h, d):
        k = (z - s if d == 0 else z + s) * NX + x
        return rcopy(half(k, h), half(k, h), zsem_s.at[s - 1, h, d], zsem_r.at[s - 1, h, d], up if d == 0 else down)

    def qzcopy(s, d):
        ref = qrow(z - s if d == 0 else z + s)
        return rcopy(ref, ref, qzs.at[s, d], qzr.at[s, d], up if d == 0 else down)

    def qzlanded(s, d):
        ref = qrow(z - s if d == 0 else z + s)
        return rcopy(ref, ref, qzs.at[s - 1, d], qzr.at[s - 1, d], up if d == 0 else down)

    def has(s, d):
        return z - s >= 0 if d == 0 else z + s <= NZ - 1

    def goes(d):
        return z < NZ - 1 if d == 0 else z > 0

    def zpass(s):
        for h in range(2):
            for d in range(2):
                @pl.when(has(s, d))
                def _():
                    zlanded(s, h, d).wait_recv()

                    @pl.when(goes(d))
                    def _():
                        zcopy(s, h, d).start()

    def qzpass(s):
        for d in range(2):
            @pl.when(has(s, d))
            def _():
                qzlanded(s, d).wait_recv()

                @pl.when(goes(d))
                def _():
                    qzcopy(s, d).start()

    def xsend(j):
        for n in (0, 2, 1, 3):
            xcopy(j, n).start()

    def xpass(j):
        for n in (0, 2):
            xlanded(j, n).wait_recv()
            xcopy(j, 4 + n // 2).start()

    def xdone(j):
        for n in (1, 3, 4, 5):
            xlanded(j, n).wait_recv()

    def multiply(k, first=False):
        part = jnp.dot(X[k], W[k], preferred_element_type=jnp.float32)
        if first:
            acc[...] = part
        else:
            acc[...] += part

    def multiply_row(j):
        r = order(j) * NX

        @pl.loop(0, NX)
        def _(n):
            multiply(r + n)

    def rs_copy(hf, d):
        t = (y + d) % NY
        return rcopy(stg.at[t, hf], rbuf.at[hf, d - 1], rss.at[hf], rsr.at[hf], isl(zh, t))

    def sc_copy(d):
        t = (y + d) % NY
        lanes = pl.ds(pl.multiple_of((t // 4) * 128, 128), 128)
        return rcopy(scbuf.at[:, lanes], rsc.at[d - 1], scs, scr, isl(zh, t))

    def zh_copies(hf):
        return (
            rcopy(zs.at[hf], zrs.at[hf], zhs.at[hf, 0], zhr.at[hf, 0], far),
            rcopy(zm.at[hf], zrm.at[hf], zhs.at[hf, 1], zhr.at[hf, 1], far),
        )

    def ag_copy(hf, d):
        return rcopy(res.at[hf, y], res.at[hf, y], ags.at[hf], agr.at[hf], isl(zh, (y + d) % NY))

    far_first = (4, 3, 5, 2, 6, 1, 7)

    def small_columns():
        rcopy(rsc, rsc, scs, scr, far).wait_recv()
        ld_ow.wait()
        lanes = pl.ds(pl.multiple_of((y // 4) * 128, 128), 128)
        tmp[...] = jnp.zeros_like(tmp)
        tmp[pl.ds(0, 4), :] = scbuf[:, lanes]
        for d in range(1, NY):
            tmp[pl.ds(4 * d, 4), :] = rsc[d - 1]
        tmp[pl.ds(32, 4), :] = owbuf[:, lanes].astype(jnp.float32)
        tmpt[...] = tmp[...].T

    def partial(hf):
        rcopy(rbuf.at[hf], rbuf.at[hf], rss.at[hf], rsr.at[hf], far).wait_recv()
        cols = tmpt[pl.ds(pl.multiple_of(32 * (y % 4) + 16 * hf, 16), 16), :]
        for b in range(4):
            lanes = pl.ds(128 * b, 128)
            total = jnp.zeros((16, 128), jnp.float32)
            held = jnp.zeros((16, 128), jnp.float32)
            own = jnp.broadcast_to(cols[:, 32 + b : 33 + b], (16, 128))
            for d in range(NY):
                if d == 0:
                    code, state = stg[y, hf, pl.ds(0, 16), lanes], stg[y, hf, pl.ds(16, 16), lanes]
                else:
                    code, state = (
                        rbuf[hf, d - 1, pl.ds(0, 16), lanes],
                        rbuf[hf, d - 1, pl.ds(16, 16), lanes],
                    )
                total += code.astype(jnp.float32) * cols[:, 4 * d + b : 4 * d + b + 1]
                who = (zh * NY + (y + NY - d) % NY).astype(jnp.float32)
                held += jnp.where(own == who, state.astype(jnp.float32), 0.0)
            zs[hf, :, lanes] = total
            zm[hf, :, lanes] = held.astype(jnp.bfloat16)
        for cp in zh_copies(hf):
            cp.start()

    def finish(hf):
        for cp in zh_copies(hf):
            cp.wait_recv()
        mean = (zs[hf] + zrs[hf]) * (1.0 / (2 * NY))
        held = zm[hf].astype(jnp.float32) + zrm[hf].astype(jnp.float32)
        fresh = outer_momentum * held + mean
        updated = gbuf[hf].astype(jnp.float32) - outer_rate * (mean + outer_momentum * fresh)
        res[hf, y, 0] = updated.astype(jnp.bfloat16)
        res[hf, y, 1] = fresh.astype(jnp.bfloat16)
        for d in far_first:
            ag_copy(hf, d).start()

    def zstart():
        for h in range(2):
            for d in range(2):
                @pl.when(goes(d))
                def _():
                    zcopy(0, h, d).start()

    def qzstart():
        for d in range(2):
            @pl.when(goes(d))
            def _():
                qzcopy(0, d).start()

    def rs_start(hf):
        for d in far_first:
            rs_copy(hf, d).start()

    def sc_start():
        for d in far_first:
            sc_copy(d).start()

    def act_start():
        @pl.loop(0, NX * NZ)
        def _(k):
            col = pl.multiple_of((2 * k + 1 - c) * depth, depth)
            rcopy(act.at[:, pl.ds(col, depth)], X.at[k, pl.ds(tok, tok), :], acts, actr, partner).start()

    act_in = rcopy(X.at[:, pl.ds(tok, tok), :], X.at[:, pl.ds(tok, tok), :], acts, actr, partner)

    def act_wait():
        act_in.wait_recv()
        pltpu.make_async_copy(X.at[:, pl.ds(0, tok), :], X.at[:, pl.ds(0, tok), :], lsem.at[6]).wait()

    def qstart():
        qxcopy(0).start()
        qxcopy(1).start()

    def qpass():
        for n in range(2):
            qxlanded(n).wait_recv()
            qxcopy(2 + n).start()

    def qdone():
        for n in (2, 3):
            qxlanded(n).wait_recv()

    def far_here():
        @pl.when(zh == 0)
        def _():
            pl.semaphore_wait(farsem, 1)

    pcopy = rcopy(acc.at[pl.ds(tok, tok), :], pacc, pts, ptr_, partner)
    res_in = [
        rcopy(res.at[hf, pl.ds(0, 7)], res.at[hf, pl.ds(0, 7)], ags.at[hf], agr.at[hf], far)
        for hf in range(2)
    ]
    outs = [
        pltpu.make_async_copy(res.at[hf, :, n], out.at[:, hf], osem.at[hf, n])
        for hf in range(2)
        for n, out in enumerate((og, om))
    ]

    def gathered(hf):
        res_in[hf].wait_recv()
        outs[2 * hf].start()
        outs[2 * hf + 1].start()

    def finish_proj():
        pcopy.wait_recv()
        proj[...] = (acc[pl.ds(0, tok), :] + pacc[...]).astype(jnp.bfloat16)

    def sent_a():
        for j in range(NZ):
            for n in range(6):
                xcopy(j, n).wait_send()
        for n in range(4):
            qxcopy(n).wait_send()
        for s in range(NZ - 1):
            for d in range(2):
                @pl.when(has(s, d) & goes(d))
                def _():
                    for h in range(2):
                        zcopy(s, h, d).wait_send()
                    qzcopy(s, d).wait_send()
        act_in.wait_send()
        pcopy.wait_send()

    def sent_b():
        rcopy(rsc, rsc, scs, scr, far).wait_send()
        for hf in range(2):
            rcopy(rbuf.at[hf], rbuf.at[hf], rss.at[hf], rsr.at[hf], far).wait_send()
            for cp in zh_copies(hf):
                cp.wait_send()
            res_in[hf].wait_send()
        for cp in outs:
            cp.wait()

    qstart()
    xsend(0)
    zstart()
    answer()
    codes_ready()
    peers_here()
    rs_start(0)
    sc_start()
    rs_start(1)
    act_start()
    x_start()
    qpass()
    zpass(1)
    xsend(1)
    xpass(0)
    qdone()
    qzstart()
    small_columns()
    far_here()
    partial(0)
    zpass(2)
    xsend(2)
    xpass(1)
    xdone(0)
    act_wait()
    acc[...] = jnp.zeros_like(acc)
    partial(1)
    zpass(3)
    xsend(3)
    multiply_row(0)
    qzpass(1)
    xpass(2)
    ld_gw.wait()
    finish(0)
    qzpass(2)
    xdone(1)
    qzpass(3)
    multiply_row(1)
    xpass(3)
    finish(1)
    xdone(2)
    multiply_row(2)
    xdone(3)
    multiply_row(3)
    pcopy.start()
    gathered(0)
    gathered(1)
    finish_proj()
    sent_a()
    sent_b()


def hand_over(*refs):
    sem = refs[6]
    copies = [pltpu.make_async_copy(refs[n], refs[n + 3], sem.at[n]) for n in range(3)]
    for cp in copies:
        cp.start()
    for cp in copies:
        cp.wait()


def body(
    activations, local_weights, grad_codes, block_scales, global_weights, momentum, block_owner
):
    tok, model = activations.shape
    rows, width = local_weights.shape[1:]
    nk = NX * NZ
    cut = (NY, 2, rows // (2 * NY), width)
    any_space = pl.BlockSpec(memory_space=pl.ANY)
    vmem = pl.BlockSpec(memory_space=pltpu.VMEM)
    hbm = functools.partial(pltpu.with_memory_space_constraint, memory_space=pltpu.HBM)
    bf, f32 = jnp.bfloat16, jnp.float32
    dma = pltpu.SemaphoreType.DMA
    proj, og, om = pl.pallas_call(
        gather_kernel,
        out_shape=(
            pltpu.VMEM((tok, width), bf),
            pltpu.VMEM(cut, bf),
            pltpu.VMEM(cut, bf),
        ),
        in_specs=[any_space] * 7,
        out_specs=(vmem, vmem, vmem),
        scratch_shapes=[
            pltpu.VMEM((nk, 2 * tok, rows), bf),
            pltpu.VMEM((nk, rows, width), bf),
            pltpu.VMEM((2 * tok, width), f32),
            pltpu.VMEM((tok, width), f32),
            pltpu.VMEM(cut, jnp.int32),
            pltpu.VMEM((NY, 2, 32, width), bf),
            pltpu.VMEM((2, NY - 1, 32, width), bf),
            pltpu.VMEM((4, rows), f32),
            pltpu.VMEM((NY - 1, 4, 128), f32),
            pltpu.VMEM((4, rows), jnp.int32),
            pltpu.VMEM((2, 16, width), bf),
            pltpu.VMEM((128, 128), f32),
            pltpu.VMEM((128, 128), f32),
            pltpu.VMEM((2, 16, width), f32),
            pltpu.VMEM((2, 16, width), bf),
            pltpu.VMEM((2, 16, width), f32),
            pltpu.VMEM((2, 16, width), bf),
            pltpu.VMEM((2, NY, 2, 16, width), bf),
            dma((7,)),
            dma((NZ, 2, 2)), dma((NZ, 2, 2)),
            dma((NZ, 6)), dma((NZ, 6)),
            dma((4,)), dma((4,)),
            dma((NZ, 2)), dma((NZ, 2)),
            dma, dma,
            dma, dma,
            dma((2,)), dma((2,)),
            dma, dma,
            dma((2, 2)), dma((2, 2)),
            dma((2,)), dma((2,)),
            dma((2, 2)),
            pltpu.SemaphoreType.REGULAR,
            pltpu.SemaphoreType.REGULAR,
        ],
        compiler_params=pltpu.CompilerParams(
            collective_id=0, has_side_effects=True, vmem_limit_bytes=48 * 2**20
        ),
        name="sync_and_project",
    )(
        hbm(activations),
        hbm(local_weights[0]),
        hbm(grad_codes[0].reshape(cut)),
        hbm(block_scales[0].T),
        hbm(block_owner.T),
        hbm(global_weights.reshape(cut)),
        hbm(momentum[0].reshape(cut)),
    )
    return pl.pallas_call(
        hand_over,
        out_shape=(
            jax.ShapeDtypeStruct((tok, width), bf),
            jax.ShapeDtypeStruct((rows, width), bf),
            jax.ShapeDtypeStruct((rows, width), bf),
        ),
        in_specs=[vmem] * 3,
        out_specs=[any_space] * 3,
        scratch_shapes=[dma((3,))],
        compiler_params=pltpu.CompilerParams(vmem_limit_bytes=16 * 2**20),
        name="hand_over",
    )(proj, og.reshape(rows, width), om.reshape(rows, width))


def solution(mesh):
    return jax.shard_map(
        body,
        mesh=mesh,
        in_specs=(
            P(("island", "fsdp"), None),
            P("island", "fsdp", None),
            P("island", "fsdp", None),
            P("island", "fsdp", None),
            P("fsdp", None),
            P("island", "fsdp", None),
            P("fsdp", None),
        ),
        out_specs=(P(("island", "fsdp"), None), P("fsdp", None), P("fsdp", None)),
        check_vma=False,
    )
```

```python
import functools

import jax
import jax.numpy as jnp
from jax import lax
from jax.experimental import pallas as pl
from jax.experimental.pallas import tpu as pltpu
from jax.sharding import PartitionSpec as P

MESH = pl.DeviceIdType.MESH

outer_momentum = 0.9
outer_rate = 0.7

NX, NZ, NY = 4, 4, 8
NQ = 4
Q = 16
QF = 1 if Q < 32 else 2


def gather_kernel(
    act, wown, codes, scales, owner, gw, mom,
    proj, res,
    X, W, acc, pacc,
    cbuf, stg, rbuf, scbuf, rsc, owbuf, gbuf, tmp, tmpt, zs, zm, zrs, zrm,
    lsem, zsem_s, zsem_r, xsem_s, xsem_r, qxs, qxr, qzs, qzr,
    acts, actr, pts, ptr_, rss, rsr, scs, scr, zhs, zhr, ags, agr, farsem, heresem,
):
    i, f = lax.axis_index("island"), lax.axis_index("fsdp")
    zh, y = i // NY, i % NY
    z, x, c = f // (2 * NX), (f // 2) % NX, f % 2
    rows = wown.shape[0]
    p = rows - Q
    cut = p // 32 * 16
    tok = act.shape[0]
    depth = rows

    def fs(zz, xx, cc):
        return {"fsdp": zz * 2 * NX + xx * 2 + cc}

    def isl(hh, yy):
        return {"island": hh * NY + yy}

    xl, xr, xo = (x + NX - 1) % NX, (x + 1) % NX, (x + 2) % NX
    right, left = fs(z, xr, c), fs(z, xl, c)
    partner = fs(z, x, 1 - c)
    far = isl(1 - zh, y)

    def rcopy(src, dst, ss, rs, dev):
        return pltpu.make_async_remote_copy(
            src_ref=src, dst_ref=dst, send_sem=ss, recv_sem=rs, device_id=dev, device_id_type=MESH
        )

    g = y // 5
    rank = (1 - g) * (2 * y - 1 + (NY - y) // NY) + g * 2 * (NY - y)

    def rank_of(t):
        gt = t // 5
        return (1 - gt) * (2 * t - 1 + (NY - t) // NY) + gt * 2 * (NY - t)

    up, down = fs(z + 1, x, c), fs(z - 1, x, c)
    bar = pltpu.get_barrier_semaphore()

    def hello(dev):
        pl.semaphore_signal(bar, inc=1, device_id=dev, device_id_type=MESH)

    ld_w = pltpu.make_async_copy(wown, W.at[z * NX + x], lsem.at[1])
    ld_w.start()
    for dev in (right, left, partner):
        hello(dev)

    @pl.when(z < NZ - 1)
    def _():
        hello(up)

    @pl.when(z > 0)
    def _():
        hello(down)

    for d in range(1, NY):
        t = (y + d) % NY

        @pl.when(rank_of(t) > rank)
        def _():
            hello(isl(zh, t))

    @pl.when(zh == 0)
    def _():
        hello(far)

    kown = z * NX + x
    ld_codes = pltpu.make_async_copy(codes, cbuf, lsem.at[0])
    ld_codes.start()
    hw = mom.shape[3] // 2
    ld_mom = [
        pltpu.make_async_copy(
            mom.at[:, :, :, pl.ds(ch * hw, hw)], stg.at[:, :, ch, pl.ds(16, 16), :], lsem.at[(2, 7)[ch]]
        )
        for ch in range(2)
    ]
    for ld in ld_mom:
        ld.start()
    ld_sc = pltpu.make_async_copy(scales, scbuf, lsem.at[3])
    ld_sc.start()
    ld_ow = pltpu.make_async_copy(owner, owbuf, lsem.at[4])
    ld_ow.start()
    ld_gw = pltpu.make_async_copy(gw.at[y], gbuf, lsem.at[5])
    ld_gw.start()

    edge = 1 - (z + 1) // NZ + (z + NZ - 1) // NZ
    ld_w.wait()
    pl.semaphore_wait(bar, 3 + edge + rank + zh)

    def answer():
        for d in range(1, NY):
            t = (y + d) % NY

            @pl.when(rank_of(t) < rank)
            def _():
                pl.semaphore_signal(heresem, inc=1, device_id=isl(zh, t), device_id_type=MESH)

        @pl.when(zh == 1)
        def _():
            pl.semaphore_signal(farsem, inc=1, device_id=far, device_id_type=MESH)

    def x_start():
        @pl.loop(0, NX * NZ)
        def _(k):
            col = pl.multiple_of((2 * k + c) * depth, depth)
            pltpu.make_async_copy(
                act.at[:, pl.ds(col, depth)], X.at[k, pl.ds(0, tok), :], lsem.at[6]
            ).start()

    def codes_ready():
        ld_codes.wait()

        @pl.loop(0, NY)
        def _(t):
            for ch in range(2):
                code = cbuf[t, :, :, pl.ds(ch * hw, hw)]
                stg[t, :, ch, pl.ds(0, 16), :] = code.astype(jnp.float32).astype(jnp.bfloat16)

        for ld in ld_mom:
            ld.wait()
        ld_sc.wait()

    def peers_here():
        @pl.when(rank < NY - 1)
        def _():
            pl.semaphore_wait(heresem, NY - 1 - rank)

    def half(k, h, at=cut):
        return W.at[k, pl.ds(h * at, at + h * (p - 2 * at)), :]

    def xhalf(j, k, h):
        return half(k, h, cut if j < NZ // 2 else p - cut)

    def qpart(k):
        return W.at[k, pl.ds(p, Q), :]

    def qhalf(k, h):
        return W.at[k, pl.ds(p + h * (Q // QF), Q // QF), :]

    def qrow(r):
        return W.at[pl.ds(r * NX, NX), pl.ds(p, Q), :]

    m = z // 2
    e = z * (1 - m) + (NZ - 1 - z) * m

    def order(j):
        g = j if j >= 2 else j * (1 - e) + (1 - j) * e
        return g * (1 - m) + (NZ - 1 - g) * m

    def xcopy(j, n):
        r = order(j) * NX
        k, h, dev = [
            (r + x, 0, right), (r + x, 1, right), (r + x, 1, left), (r + x, 0, left),
            (r + xl, 0, right), (r + xr, 1, left),
        ][n]
        return rcopy(xhalf(j, k, h), xhalf(j, k, h), xsem_s.at[j, n], xsem_r.at[j, n], dev)

    def xlanded(j, n):
        r = order(j) * NX
        k, h = [(r + xl, 0), (r + xl, 1), (r + xr, 1), (r + xr, 0), (r + xo, 0), (r + xo, 1)][n]
        return rcopy(xhalf(j, k, h), xhalf(j, k, h), xsem_s.at[j, n], xsem_r.at[j, n], right)

    def qxcopy(n):
        k = [kown, kown, z * NX + xl, z * NX + xr][n]
        dev = [right, left, right, left][n]
        ref = qpart(k) if n < 2 else qhalf(k, n - 2)
        return rcopy(ref, ref, qxs.at[n], qxr.at[n], dev)

    def qxlanded(n):
        k = z * NX + [xl, xr, xo, xo][n]
        ref = qpart(k) if n < 2 else qhalf(k, n - 2)
        return rcopy(ref, ref, qxs.at[n], qxr.at[n], right)

    def zcopy(s, h, d):
        k = (z - s if d == 0 else z + s) * NX + x
        return rcopy(half(k, h), half(k, h), zsem_s.at[s, h, d], zsem_r.at[s, h, d], up if d == 0 else down)

    def zlanded(s, h, d):
        k = (z - s if d == 0 else z + s) * NX + x
        return rcopy(half(k, h), half(k, h), zsem_s.at[s - 1, h, d], zsem_r.at[s - 1, h, d], up if d == 0 else down)

    def qzcopy(s, d):
        ref = qrow(z - s if d == 0 else z + s)
        return rcopy(ref, ref, qzs.at[s, d], qzr.at[s, d], up if d == 0 else down)

    def qzlanded(s, d):
        ref = qrow(z - s if d == 0 else z + s)
        return rcopy(ref, ref, qzs.at[s - 1, d], qzr.at[s - 1, d], up if d == 0 else down)

    def has(s, d):
        return z - s >= 0 if d == 0 else z + s <= NZ - 1

    def goes(d):
        return z < NZ - 1 if d == 0 else z > 0

    def zpass(s):
        for h in range(2):
            for d in range(2):
                @pl.when(has(s, d))
                def _():
                    zlanded(s, h, d).wait_recv()

                    @pl.when(goes(d))
                    def _():
                        zcopy(s, h, d).start()

    def qzpass(s):
        for d in range(2):
            @pl.when(has(s, d))
            def _():
                qzlanded(s, d).wait_recv()

                @pl.when(goes(d))
                def _():
                    qzcopy(s, d).start()

    def xsend(j):
        for n in (0, 2, 1, 3):
            xcopy(j, n).start()

    def xpass(j):
        for n in (0, 2):
            xlanded(j, n).wait_recv()
            xcopy(j, 4 + n // 2).start()

    def xdone(j):
        for n in (1, 3, 4, 5):
            xlanded(j, n).wait_recv()

    def multiply(k, first=False):
        part = jnp.dot(X[k], W[k], preferred_element_type=jnp.float32)
        if first:
            acc[...] = part
        else:
            acc[...] += part

    def multiply_row(j):
        r = order(j) * NX

        @pl.loop(0, NX)
        def _(n):
            multiply(r + n)

    def last_row():
        r = order(NZ - 1) * NX
        multiply(r + x)
        for n in (1, 3):
            xlanded(NZ - 1, n).wait_recv()
        multiply(r + xl)
        multiply(r + xr)
        for n in (4, 5):
            xlanded(NZ - 1, n).wait_recv()
        acc[pl.ds(tok, tok), :] += jnp.dot(
            X[r + xo, pl.ds(tok, tok), :], W[r + xo], preferred_element_type=jnp.float32
        )

    def last_own():
        r = order(NZ - 1) * NX
        acc[pl.ds(0, tok), :] += jnp.dot(
            X[r + xo, pl.ds(0, tok), :], W[r + xo], preferred_element_type=jnp.float32
        )

    def rs_copy(q, d):
        t = (y + d) % NY
        return rcopy(stg.at[t, q // 2, q % 2], rbuf.at[q, d - 1], rss.at[q], rsr.at[q], isl(zh, t))

    def sc_copy(d):
        t = (y + d) % NY
        lanes = pl.ds(pl.multiple_of((t // 4) * 128, 128), 128)
        return rcopy(scbuf.at[:, lanes], rsc.at[d - 1], scs, scr, isl(zh, t))

    def zh_copies(q):
        return (
            rcopy(zs.at[q], zrs.at[q], zhs.at[q, 0], zhr.at[q, 0], far),
            rcopy(zm.at[q], zrm.at[q], zhs.at[q, 1], zhr.at[q, 1], far),
        )

    def ag_copy(q, d):
        return rcopy(res.at[q, y], res.at[q, y], ags.at[q], agr.at[q], isl(zh, (y + d) % NY))

    far_first = (4, 3, 5, 2, 6, 1, 7)

    def small_columns():
        rcopy(rsc, rsc, scs, scr, far).wait_recv()
        ld_ow.wait()
        lanes = pl.ds(pl.multiple_of((y // 4) * 128, 128), 128)
        tmp[...] = jnp.zeros_like(tmp)
        tmp[pl.ds(0, 4), :] = scbuf[:, lanes]
        for d in range(1, NY):
            tmp[pl.ds(4 * d, 4), :] = rsc[d - 1]
        tmp[pl.ds(32, 4), :] = owbuf[:, lanes].astype(jnp.float32)
        tmpt[...] = tmp[...].T

    def partial(q):
        rcopy(rbuf.at[q], rbuf.at[q], rss.at[q], rsr.at[q], far).wait_recv()
        cols = tmpt[pl.ds(pl.multiple_of(32 * (y % 4) + 16 * (q // 2), 16), 16), :]
        for n in range(2):
            lanes = pl.ds(128 * n, 128)
            b = 2 * (q % 2) + n
            total = jnp.zeros((16, 128), jnp.float32)
            held = jnp.zeros((16, 128), jnp.float32)
            own = jnp.broadcast_to(cols[:, 32 + b : 33 + b], (16, 128))
            for d in range(NY):
                if d == 0:
                    code, state = (
                        stg[y, q // 2, q % 2, pl.ds(0, 16), lanes],
                        stg[y, q // 2, q % 2, pl.ds(16, 16), lanes],
                    )
                else:
                    code, state = (
                        rbuf[q, d - 1, pl.ds(0, 16), lanes],
                        rbuf[q, d - 1, pl.ds(16, 16), lanes],
                    )
                total += code.astype(jnp.float32) * cols[:, 4 * d + b : 4 * d + b + 1]
                who = (zh * NY + (y + NY - d) % NY).astype(jnp.float32)
                held += jnp.where(own == who, state.astype(jnp.float32), 0.0)
            zs[q, :, lanes] = total
            zm[q, :, lanes] = held.astype(jnp.bfloat16)
        for cp in zh_copies(q):
            cp.start()

    def finish(q):
        for cp in zh_copies(q):
            cp.wait_recv()
        mean = (zs[q] + zrs[q]) * (1.0 / (2 * NY))
        held = zm[q].astype(jnp.float32) + zrm[q].astype(jnp.float32)
        fresh = outer_momentum * held + mean
        old = gbuf[q // 2, :, pl.ds((q % 2) * hw, hw)].astype(jnp.float32)
        updated = old - outer_rate * (mean + outer_momentum * fresh)
        res[q, y, 0] = updated.astype(jnp.bfloat16)
        res[q, y, 1] = fresh.astype(jnp.bfloat16)
        for d in far_first:
            ag_copy(q, d).start()

    def zstart():
        for h in range(2):
            for d in range(2):
                @pl.when(goes(d))
                def _():
                    zcopy(0, h, d).start()

    def qzstart():
        for d in range(2):
            @pl.when(goes(d))
            def _():
                qzcopy(0, d).start()

    def rs_start(q):
        if q == 0:
            for d in far_first:
                sc_copy(d).start()
        for d in far_first:
            rs_copy(q, d).start()

    def act_start():
        @pl.loop(0, NX * NZ)
        def _(k):
            col = pl.multiple_of((2 * k + 1 - c) * depth, depth)
            rcopy(act.at[:, pl.ds(col, depth)], X.at[k, pl.ds(tok, tok), :], acts, actr, partner).start()

    act_in = rcopy(X.at[:, pl.ds(tok, tok), :], X.at[:, pl.ds(tok, tok), :], acts, actr, partner)

    def act_wait():
        act_in.wait_recv()
        pltpu.make_async_copy(X.at[:, pl.ds(0, tok), :], X.at[:, pl.ds(0, tok), :], lsem.at[6]).wait()

    def qstart():
        qxcopy(0).start()
        qxcopy(1).start()

    def qpass():
        for n in range(2):
            qxlanded(n).wait_recv()
            if n < QF:
                qxcopy(2 + n).start()

    def qdone():
        for n in range(QF):
            qxlanded(2 + n).wait_recv()

    def far_here():
        pl.semaphore_wait(farsem, 1)

    pcopy = rcopy(acc.at[pl.ds(tok, tok), :], pacc, pts, ptr_, partner)
    res_in = [
        rcopy(res.at[q, pl.ds(0, 7)], res.at[q, pl.ds(0, 7)], ags.at[q], agr.at[q], far)
        for q in range(NQ)
    ]

    def gathered(q):
        res_in[q].wait_recv()

    def finish_proj():
        pcopy.wait_recv()
        proj[...] = (acc[pl.ds(0, tok), :] + pacc[...]).astype(jnp.bfloat16)

    def sent_a():
        for j in range(NZ):
            for n in range(6):
                xcopy(j, n).wait_send()
        for n in range(2 + QF):
            qxcopy(n).wait_send()
        for s in range(NZ - 1):
            for d in range(2):
                @pl.when(has(s, d) & goes(d))
                def _():
                    for h in range(2):
                        zcopy(s, h, d).wait_send()
                    qzcopy(s, d).wait_send()
        act_in.wait_send()
        pcopy.wait_send()

    def sent_b():
        rcopy(rsc, rsc, scs, scr, far).wait_send()
        for q in range(NQ):
            rcopy(rbuf.at[q], rbuf.at[q], rss.at[q], rsr.at[q], far).wait_send()
            for cp in zh_copies(q):
                cp.wait_send()
            res_in[q].wait_send()

    qstart()
    xsend(0)
    zstart()
    answer()
    codes_ready()
    act_start()
    x_start()
    @pl.when(zh == 1)
    def _():
        peers_here()

    @pl.when(zh == 1)
    def _():
        rs_start(0)
        rs_start(1)
        rs_start(2)
        rs_start(3)

    qpass()
    zpass(1)
    xsend(1)
    @pl.when(zh == 0)
    def _():
        peers_here()

    @pl.when(zh == 0)
    def _():
        rs_start(0)
        rs_start(1)
        rs_start(2)
        rs_start(3)

    xpass(0)
    qdone()
    qzstart()
    @pl.when(zh == 1)
    def _():
        small_columns()
        partial(0)
        partial(1)

    zpass(2)
    xsend(2)
    @pl.when(zh == 1)
    def _():
        partial(2)

    xpass(1)
    qzpass(1)
    @pl.when(zh == 1)
    def _():
        partial(3)

    @pl.when(zh == 0)
    def _():
        far_here()

    @pl.when(zh == 0)
    def _():
        small_columns()
        partial(0)
        partial(1)
        partial(2)

    xdone(0)
    act_wait()
    acc[...] = jnp.zeros_like(acc)
    multiply_row(0)
    ld_gw.wait()
    finish(0)
    @pl.when(zh == 0)
    def _():
        partial(3)

    zpass(3)
    xsend(3)
    xpass(2)
    qzpass(2)
    finish(1)
    qzpass(3)
    xdone(1)
    multiply_row(1)
    finish(2)
    xpass(3)
    finish(3)
    xdone(2)
    multiply_row(2)
    last_row()
    pcopy.start()
    last_own()
    for q in range(NQ):
        gathered(q)
    finish_proj()
    sent_a()
    sent_b()


def hand_over(proj, res, out, og, om, sem):
    hw = res.shape[4]
    copies = [pltpu.make_async_copy(proj, out, sem.at[0])]
    for n, held in enumerate((og, om)):
        for q in range(NQ):
            part = held.at[:, q // 2, :, pl.ds(q % 2 * hw, hw)]
            copies.append(pltpu.make_async_copy(res.at[q, :, n], part, sem.at[1 + NQ * n + q]))
    for cp in copies:
        cp.start()
    for cp in copies:
        cp.wait()


def body(
    activations, local_weights, grad_codes, block_scales, global_weights, momentum, block_owner
):
    tok, model = activations.shape
    rows, width = local_weights.shape[1:]
    nk = NX * NZ
    cut = (NY, 2, rows // (2 * NY), width)
    any_space = pl.BlockSpec(memory_space=pl.ANY)
    vmem = pl.BlockSpec(memory_space=pltpu.VMEM)
    hbm = functools.partial(pltpu.with_memory_space_constraint, memory_space=pltpu.HBM)
    bf, f32 = jnp.bfloat16, jnp.float32
    dma = pltpu.SemaphoreType.DMA
    proj, res = pl.pallas_call(
        gather_kernel,
        out_shape=(
            pltpu.VMEM((tok, width), bf),
            pltpu.VMEM((NQ, NY, 2, 16, width // 2), bf),
        ),
        in_specs=[any_space] * 7,
        out_specs=(vmem, vmem),
        scratch_shapes=[
            pltpu.VMEM((nk, 2 * tok, rows), bf),
            pltpu.VMEM((nk, rows, width), bf),
            pltpu.VMEM((2 * tok, width), f32),
            pltpu.VMEM((tok, width), f32),
            pltpu.VMEM(cut, jnp.int32),
            pltpu.VMEM((NY, 2, 2, 32, width // 2), bf),
            pltpu.VMEM((NQ, NY - 1, 32, width // 2), bf),
            pltpu.VMEM((4, rows), f32),
            pltpu.VMEM((NY - 1, 4, 128), f32),
            pltpu.VMEM((4, rows), jnp.int32),
            pltpu.VMEM((2, 16, width), bf),
            pltpu.VMEM((128, 128), f32),
            pltpu.VMEM((128, 128), f32),
            pltpu.VMEM((NQ, 16, width // 2), f32),
            pltpu.VMEM((NQ, 16, width // 2), bf),
            pltpu.VMEM((NQ, 16, width // 2), f32),
            pltpu.VMEM((NQ, 16, width // 2), bf),
            dma((8,)),
            dma((NZ, 2, 2)), dma((NZ, 2, 2)),
            dma((NZ, 6)), dma((NZ, 6)),
            dma((4,)), dma((4,)),
            dma((NZ, 2)), dma((NZ, 2)),
            dma, dma,
            dma, dma,
            dma((NQ,)), dma((NQ,)),
            dma, dma,
            dma((NQ, 2)), dma((NQ, 2)),
            dma((NQ,)), dma((NQ,)),
            pltpu.SemaphoreType.REGULAR,
            pltpu.SemaphoreType.REGULAR,
        ],
        compiler_params=pltpu.CompilerParams(
            collective_id=0, has_side_effects=True, vmem_limit_bytes=48 * 2**20
        ),
        name="sync_and_project",
    )(
        hbm(activations),
        hbm(local_weights[0]),
        hbm(grad_codes[0].reshape(cut)),
        hbm(block_scales[0].T),
        hbm(block_owner.T),
        hbm(global_weights.reshape(cut)),
        hbm(momentum[0].reshape(cut)),
    )
    proj, og, om = pl.pallas_call(
        hand_over,
        out_shape=(
            jax.ShapeDtypeStruct((tok, width), bf),
            jax.ShapeDtypeStruct(cut, bf),
            jax.ShapeDtypeStruct(cut, bf),
        ),
        in_specs=[vmem] * 2,
        out_specs=[any_space] * 3,
        scratch_shapes=[dma((1 + 2 * NQ,))],
        compiler_params=pltpu.CompilerParams(vmem_limit_bytes=16 * 2**20),
        name="hand_over",
    )(proj, res)
    return proj, og.reshape(rows, width), om.reshape(rows, width)


def solution(mesh):
    return jax.shard_map(
        body,
        mesh=mesh,
        in_specs=(
            P(("island", "fsdp"), None),
            P("island", "fsdp", None),
            P("island", "fsdp", None),
            P("island", "fsdp", None),
            P("fsdp", None),
            P("island", "fsdp", None),
            P("fsdp", None),
        ),
        out_specs=(P(("island", "fsdp"), None), P("fsdp", None), P("fsdp", None)),
        check_vma=False,
    )
```

```python
import functools

import jax
import jax.numpy as jnp
from jax import lax
from jax.experimental import pallas as pl
from jax.experimental.pallas import tpu as pltpu
from jax.sharding import PartitionSpec as P

MESH = pl.DeviceIdType.MESH

outer_momentum = 0.9
outer_rate = 0.7

NX, NZ, NY = 4, 4, 8
NQ = 4
Q = 32
QF = 1 if Q < 32 else 2


def gather_kernel(
    act, wown, codes, scales, owner, gw, mom,
    proj, res,
    X, W, acc, pacc,
    cbuf, stg, rbuf, scbuf, rsc, owbuf, gbuf, tmp, tmpt, zs, zm, zrs, zrm,
    lsem, zsem_s, zsem_r, xsem_s, xsem_r, qxs, qxr, qzs, qzr,
    acts, actr, pts, ptr_, rss, rsr, scs, scr, zhs, zhr, ags, agr, farsem, heresem, upsem,
):
    i, f = lax.axis_index("island"), lax.axis_index("fsdp")
    zh, y = i // NY, i % NY
    z, x, c = f // (2 * NX), (f // 2) % NX, f % 2
    rows = wown.shape[0]
    p = rows - Q
    cut = p // 32 * 16
    tok = act.shape[0]
    depth = rows

    def fs(zz, xx, cc):
        return {"fsdp": zz * 2 * NX + xx * 2 + cc}

    def isl(hh, yy):
        return {"island": hh * NY + yy}

    xl, xr, xo = (x + NX - 1) % NX, (x + 1) % NX, (x + 2) % NX
    right, left = fs(z, xr, c), fs(z, xl, c)
    partner = fs(z, x, 1 - c)
    far = isl(1 - zh, y)

    def rcopy(src, dst, ss, rs, dev):
        return pltpu.make_async_remote_copy(
            src_ref=src, dst_ref=dst, send_sem=ss, recv_sem=rs, device_id=dev, device_id_type=MESH
        )

    g = y // 5
    rank = (1 - g) * (2 * y - 1 + (NY - y) // NY) + g * 2 * (NY - y)

    def rank_of(t):
        gt = t // 5
        return (1 - gt) * (2 * t - 1 + (NY - t) // NY) + gt * 2 * (NY - t)

    up, down = fs(z + 1, x, c), fs(z - 1, x, c)
    bar = pltpu.get_barrier_semaphore()

    def hello(dev):
        pl.semaphore_signal(bar, inc=1, device_id=dev, device_id_type=MESH)

    ld_w = pltpu.make_async_copy(wown, W.at[z * NX + x], lsem.at[1])
    ld_w.start()
    for dev in (right, left, partner):
        hello(dev)

    @pl.when(z < NZ - 1)
    def _():
        hello(up)

    for d in range(1, NY):
        t = (y + d) % NY

        @pl.when(rank_of(t) > rank)
        def _():
            hello(isl(zh, t))

    @pl.when(zh == 0)
    def _():
        hello(far)

    kown = z * NX + x
    ld_codes = pltpu.make_async_copy(codes, cbuf, lsem.at[0])
    ld_codes.start()
    hw = mom.shape[3] // 2
    ld_mom = [
        pltpu.make_async_copy(
            mom.at[:, :, :, pl.ds(ch * hw, hw)], stg.at[:, :, ch, pl.ds(16, 16), :], lsem.at[(2, 7)[ch]]
        )
        for ch in range(2)
    ]
    for ld in ld_mom:
        ld.start()
    ld_sc = pltpu.make_async_copy(scales, scbuf, lsem.at[3])
    ld_sc.start()
    ld_ow = pltpu.make_async_copy(owner, owbuf, lsem.at[4])
    ld_ow.start()
    ld_gw = pltpu.make_async_copy(gw.at[y], gbuf, lsem.at[5])
    ld_gw.start()

    below = (z + NZ - 1) // NZ
    ld_w.wait()
    pl.semaphore_wait(bar, 3 + below + rank + zh)

    def zanswer():
        @pl.when(z > 0)
        def _():
            pl.semaphore_signal(upsem, inc=1, device_id=down, device_id_type=MESH)

    def answer():
        for d in range(1, NY):
            t = (y + d) % NY

            @pl.when(rank_of(t) < rank)
            def _():
                pl.semaphore_signal(heresem, inc=1, device_id=isl(zh, t), device_id_type=MESH)

        @pl.when(zh == 1)
        def _():
            pl.semaphore_signal(farsem, inc=1, device_id=far, device_id_type=MESH)

    def x_start():
        @pl.loop(0, NX * NZ)
        def _(k):
            col = pl.multiple_of((2 * k + c) * depth, depth)
            pltpu.make_async_copy(
                act.at[:, pl.ds(col, depth)], X.at[k, pl.ds(0, tok), :], lsem.at[6]
            ).start()

    def codes_ready():
        ld_codes.wait()

        @pl.loop(0, NY)
        def _(t):
            for ch in range(2):
                code = cbuf[t, :, :, pl.ds(ch * hw, hw)]
                stg[t, :, ch, pl.ds(0, 16), :] = code.astype(jnp.float32).astype(jnp.bfloat16)

        for ld in ld_mom:
            ld.wait()
        ld_sc.wait()

    def peers_here():
        @pl.when(rank < NY - 1)
        def _():
            pl.semaphore_wait(heresem, NY - 1 - rank)

    def half(k, h, at=cut):
        return W.at[k, pl.ds(h * at, at + h * (p - 2 * at)), :]

    def xhalf(j, k, h):
        return half(k, h, cut if j < NZ // 2 else p - cut)

    def qpart(k):
        return W.at[k, pl.ds(p, Q), :]

    def qhalf(k, h):
        return W.at[k, pl.ds(p + h * (Q // QF), Q // QF), :]

    def qrow(r):
        return W.at[pl.ds(r * NX, NX), pl.ds(p, Q), :]

    m = z // 2
    e = z * (1 - m) + (NZ - 1 - z) * m

    def order(j):
        g = j if j >= 2 else j * (1 - e) + (1 - j) * e
        return g * (1 - m) + (NZ - 1 - g) * m

    def xcopy(j, n):
        r = order(j) * NX
        k, h, dev = [
            (r + x, 0, right), (r + x, 1, right), (r + x, 1, left), (r + x, 0, left),
            (r + xl, 0, right), (r + xr, 1, left),
        ][n]
        return rcopy(xhalf(j, k, h), xhalf(j, k, h), xsem_s.at[j, n], xsem_r.at[j, n], dev)

    def xlanded(j, n):
        r = order(j) * NX
        k, h = [(r + xl, 0), (r + xl, 1), (r + xr, 1), (r + xr, 0), (r + xo, 0), (r + xo, 1)][n]
        return rcopy(xhalf(j, k, h), xhalf(j, k, h), xsem_s.at[j, n], xsem_r.at[j, n], right)

    def qxcopy(n):
        k = [kown, kown, z * NX + xl, z * NX + xr][n]
        dev = [right, left, right, left][n]
        ref = qpart(k) if n < 2 else qhalf(k, n - 2)
        return rcopy(ref, ref, qxs.at[n], qxr.at[n], dev)

    def qxlanded(n):
        k = z * NX + [xl, xr, xo, xo][n]
        ref = qpart(k) if n < 2 else qhalf(k, n - 2)
        return rcopy(ref, ref, qxs.at[n], qxr.at[n], right)

    def zcopy(s, h, d):
        k = (z - s if d == 0 else z + s) * NX + x
        return rcopy(half(k, h), half(k, h), zsem_s.at[s, h, d], zsem_r.at[s, h, d], up if d == 0 else down)

    def zlanded(s, h, d):
        k = (z - s if d == 0 else z + s) * NX + x
        return rcopy(half(k, h), half(k, h), zsem_s.at[s - 1, h, d], zsem_r.at[s - 1, h, d], up if d == 0 else down)

    def qzcopy(s, d):
        ref = qrow(z - s if d == 0 else z + s)
        return rcopy(ref, ref, qzs.at[s, d], qzr.at[s, d], up if d == 0 else down)

    def qzlanded(s, d):
        ref = qrow(z - s if d == 0 else z + s)
        return rcopy(ref, ref, qzs.at[s - 1, d], qzr.at[s - 1, d], up if d == 0 else down)

    def has(s, d):
        return z - s >= 0 if d == 0 else z + s <= NZ - 1

    def goes(d):
        return z < NZ - 1 if d == 0 else z > 0

    def zpass(s):
        for h in range(2):
            for d in range(2):
                @pl.when(has(s, d))
                def _():
                    zlanded(s, h, d).wait_recv()

                    @pl.when(goes(d))
                    def _():
                        zcopy(s, h, d).start()

    def qzpass(s):
        for d in range(2):
            @pl.when(has(s, d))
            def _():
                qzlanded(s, d).wait_recv()

                @pl.when(goes(d))
                def _():
                    qzcopy(s, d).start()

    def xsend(j):
        for n in (0, 2, 1, 3):
            xcopy(j, n).start()

    def xpass(j):
        for n in (0, 2):
            xlanded(j, n).wait_recv()
            xcopy(j, 4 + n // 2).start()

    def xdone(j):
        for n in (1, 3, 4, 5):
            xlanded(j, n).wait_recv()

    def multiply(k, first=False):
        part = jnp.dot(X[k], W[k], preferred_element_type=jnp.float32)
        if first:
            acc[...] = part
        else:
            acc[...] += part

    def multiply_row(j):
        r = order(j) * NX

        @pl.loop(0, NX)
        def _(n):
            multiply(r + n)

    def last_row():
        r = order(NZ - 1) * NX
        multiply(r + x)
        for n in (1, 3):
            xlanded(NZ - 1, n).wait_recv()
        multiply(r + xl)
        multiply(r + xr)
        for n in (4, 5):
            xlanded(NZ - 1, n).wait_recv()
        acc[pl.ds(tok, tok), :] += jnp.dot(
            X[r + xo, pl.ds(tok, tok), :], W[r + xo], preferred_element_type=jnp.float32
        )

    def last_own():
        r = order(NZ - 1) * NX
        acc[pl.ds(0, tok), :] += jnp.dot(
            X[r + xo, pl.ds(0, tok), :], W[r + xo], preferred_element_type=jnp.float32
        )

    def rs_copy(q, d):
        t = (y + d) % NY
        return rcopy(stg.at[t, q // 2, q % 2], rbuf.at[q, d - 1], rss.at[q], rsr.at[q], isl(zh, t))

    def sc_copy(d):
        t = (y + d) % NY
        lanes = pl.ds(pl.multiple_of((t // 4) * 128, 128), 128)
        return rcopy(scbuf.at[:, lanes], rsc.at[d - 1], scs, scr, isl(zh, t))

    def zh_copies(q):
        return (
            rcopy(zs.at[q], zrs.at[q], zhs.at[q, 0], zhr.at[q, 0], far),
            rcopy(zm.at[q], zrm.at[q], zhs.at[q, 1], zhr.at[q, 1], far),
        )

    def ag_copy(q, d):
        return rcopy(res.at[q, y], res.at[q, y], ags.at[q], agr.at[q], isl(zh, (y + d) % NY))

    far_first = (4, 3, 5, 2, 6, 1, 7)

    def small_columns():
        rcopy(rsc, rsc, scs, scr, far).wait_recv()
        ld_ow.wait()
        lanes = pl.ds(pl.multiple_of((y // 4) * 128, 128), 128)
        tmp[...] = jnp.zeros_like(tmp)
        tmp[pl.ds(0, 4), :] = scbuf[:, lanes]
        for d in range(1, NY):
            tmp[pl.ds(4 * d, 4), :] = rsc[d - 1]
        tmp[pl.ds(32, 4), :] = owbuf[:, lanes].astype(jnp.float32)
        tmpt[...] = tmp[...].T

    def partial(q):
        rcopy(rbuf.at[q], rbuf.at[q], rss.at[q], rsr.at[q], far).wait_recv()
        cols = tmpt[pl.ds(pl.multiple_of(32 * (y % 4) + 16 * (q // 2), 16), 16), :]
        for n in range(2):
            lanes = pl.ds(128 * n, 128)
            b = 2 * (q % 2) + n
            total = jnp.zeros((16, 128), jnp.float32)
            held = jnp.zeros((16, 128), jnp.float32)
            own = jnp.broadcast_to(cols[:, 32 + b : 33 + b], (16, 128))
            for d in range(NY):
                if d == 0:
                    code, state = (
                        stg[y, q // 2, q % 2, pl.ds(0, 16), lanes],
                        stg[y, q // 2, q % 2, pl.ds(16, 16), lanes],
                    )
                else:
                    code, state = (
                        rbuf[q, d - 1, pl.ds(0, 16), lanes],
                        rbuf[q, d - 1, pl.ds(16, 16), lanes],
                    )
                total += code.astype(jnp.float32) * cols[:, 4 * d + b : 4 * d + b + 1]
                who = (zh * NY + (y + NY - d) % NY).astype(jnp.float32)
                held += jnp.where(own == who, state.astype(jnp.float32), 0.0)
            zs[q, :, lanes] = total
            zm[q, :, lanes] = held.astype(jnp.bfloat16)
        for cp in zh_copies(q):
            cp.start()

    def finish(q):
        for cp in zh_copies(q):
            cp.wait_recv()
        mean = (zs[q] + zrs[q]) * (1.0 / (2 * NY))
        held = zm[q].astype(jnp.float32) + zrm[q].astype(jnp.float32)
        fresh = outer_momentum * held + mean
        old = gbuf[q // 2, :, pl.ds((q % 2) * hw, hw)].astype(jnp.float32)
        updated = old - outer_rate * (mean + outer_momentum * fresh)
        res[q, y, 0] = updated.astype(jnp.bfloat16)
        res[q, y, 1] = fresh.astype(jnp.bfloat16)
        for d in far_first:
            ag_copy(q, d).start()

    def zstart(d):
        @pl.when(goes(d))
        def _():
            if d == 0:
                pl.semaphore_wait(upsem, 1)
            for h in range(2):
                zcopy(0, h, d).start()

    def qzstart():
        for d in range(2):
            @pl.when(goes(d))
            def _():
                qzcopy(0, d).start()

    def rs_start(q):
        if q == 0:
            for d in far_first:
                sc_copy(d).start()
        for d in far_first:
            rs_copy(q, d).start()

    def act_start():
        @pl.loop(0, NX * NZ)
        def _(k):
            col = pl.multiple_of((2 * k + 1 - c) * depth, depth)
            rcopy(act.at[:, pl.ds(col, depth)], X.at[k, pl.ds(tok, tok), :], acts, actr, partner).start()

    act_in = rcopy(X.at[:, pl.ds(tok, tok), :], X.at[:, pl.ds(tok, tok), :], acts, actr, partner)

    def act_wait():
        act_in.wait_recv()
        pltpu.make_async_copy(X.at[:, pl.ds(0, tok), :], X.at[:, pl.ds(0, tok), :], lsem.at[6]).wait()

    def qstart():
        qxcopy(0).start()
        qxcopy(1).start()

    def qpass():
        for n in range(2):
            qxlanded(n).wait_recv()
            if n < QF:
                qxcopy(2 + n).start()

    def qdone():
        for n in range(QF):
            qxlanded(2 + n).wait_recv()

    def far_here():
        pl.semaphore_wait(farsem, 1)

    pcopy = rcopy(acc.at[pl.ds(tok, tok), :], pacc, pts, ptr_, partner)
    res_in = [
        rcopy(res.at[q, pl.ds(0, 7)], res.at[q, pl.ds(0, 7)], ags.at[q], agr.at[q], far)
        for q in range(NQ)
    ]

    def gathered(q):
        res_in[q].wait_recv()

    def finish_proj():
        pcopy.wait()
        proj[...] = (acc[pl.ds(0, tok), :] + pacc[...]).astype(jnp.bfloat16)

    def sent_a():
        for j in range(NZ):
            for n in range(6):
                xcopy(j, n).wait_send()
        for n in range(2 + QF):
            qxcopy(n).wait_send()
        for s in range(NZ - 1):
            for d in range(2):
                @pl.when(has(s, d) & goes(d))
                def _():
                    for h in range(2):
                        zcopy(s, h, d).wait_send()
                    qzcopy(s, d).wait_send()
        act_in.wait_send()

    def sent_b():
        rcopy(rsc, rsc, scs, scr, far).wait_send()
        for q in range(NQ):
            rcopy(rbuf.at[q], rbuf.at[q], rss.at[q], rsr.at[q], far).wait_send()
            for cp in zh_copies(q):
                cp.wait_send()
            res_in[q].wait_send()

    qstart()
    xsend(0)
    zanswer()
    zstart(1)
    answer()
    codes_ready()
    act_start()
    x_start()
    zstart(0)
    @pl.when(zh == 1)
    def _():
        peers_here()

    @pl.when(zh == 1)
    def _():
        rs_start(0)
        rs_start(1)
        rs_start(2)
        rs_start(3)

    qpass()
    @pl.when(zh == 0)
    def _():
        peers_here()

    @pl.when(zh == 0)
    def _():
        rs_start(0)
        rs_start(1)
        rs_start(2)
        rs_start(3)

    zpass(1)
    xsend(1)
    xpass(0)
    qdone()
    qzstart()
    @pl.when(zh == 1)
    def _():
        small_columns()
        partial(0)
        partial(1)
        partial(2)

    zpass(2)
    xsend(2)
    @pl.when(zh == 1)
    def _():
        partial(3)

    xpass(1)
    qzpass(1)
    @pl.when(zh == 0)
    def _():
        far_here()

    @pl.when(zh == 0)
    def _():
        small_columns()
        partial(0)
        partial(1)
        partial(2)

    xdone(0)
    act_wait()
    acc[...] = jnp.zeros_like(acc)
    multiply_row(0)
    ld_gw.wait()
    finish(0)
    @pl.when(zh == 0)
    def _():
        partial(3)

    zpass(3)
    xsend(3)
    xpass(2)
    qzpass(2)
    finish(1)
    xdone(1)
    multiply_row(1)
    finish(2)
    xpass(3)
    finish(3)
    xdone(2)
    multiply_row(2)
    qzpass(3)
    last_row()
    pcopy.start()
    last_own()
    for q in range(NQ):
        gathered(q)
    sent_a()
    sent_b()
    finish_proj()


def hand_over(proj, res, out, og, om, sem):
    hw = res.shape[4]
    copies = [pltpu.make_async_copy(proj, out, sem.at[0])]
    for n, held in enumerate((og, om)):
        for q in range(NQ):
            part = held.at[:, q // 2, :, pl.ds(q % 2 * hw, hw)]
            copies.append(pltpu.make_async_copy(res.at[q, :, n], part, sem.at[1 + NQ * n + q]))
    for cp in copies:
        cp.start()
    for cp in copies:
        cp.wait()


def body(
    activations, local_weights, grad_codes, block_scales, global_weights, momentum, block_owner
):
    tok, model = activations.shape
    rows, width = local_weights.shape[1:]
    nk = NX * NZ
    cut = (NY, 2, rows // (2 * NY), width)
    any_space = pl.BlockSpec(memory_space=pl.ANY)
    vmem = pl.BlockSpec(memory_space=pltpu.VMEM)
    hbm = functools.partial(pltpu.with_memory_space_constraint, memory_space=pltpu.HBM)
    bf, f32 = jnp.bfloat16, jnp.float32
    dma = pltpu.SemaphoreType.DMA
    proj, res = pl.pallas_call(
        gather_kernel,
        out_shape=(
            pltpu.VMEM((tok, width), bf),
            pltpu.VMEM((NQ, NY, 2, 16, width // 2), bf),
        ),
        in_specs=[any_space] * 7,
        out_specs=(vmem, vmem),
        scratch_shapes=[
            pltpu.VMEM((nk, 2 * tok, rows), bf),
            pltpu.VMEM((nk, rows, width), bf),
            pltpu.VMEM((2 * tok, width), f32),
            pltpu.VMEM((tok, width), f32),
            pltpu.VMEM(cut, jnp.int32),
            pltpu.VMEM((NY, 2, 2, 32, width // 2), bf),
            pltpu.VMEM((NQ, NY - 1, 32, width // 2), bf),
            pltpu.VMEM((4, rows), f32),
            pltpu.VMEM((NY - 1, 4, 128), f32),
            pltpu.VMEM((4, rows), jnp.int32),
            pltpu.VMEM((2, 16, width), bf),
            pltpu.VMEM((128, 128), f32),
            pltpu.VMEM((128, 128), f32),
            pltpu.VMEM((NQ, 16, width // 2), f32),
            pltpu.VMEM((NQ, 16, width // 2), bf),
            pltpu.VMEM((NQ, 16, width // 2), f32),
            pltpu.VMEM((NQ, 16, width // 2), bf),
            dma((8,)),
            dma((NZ, 2, 2)), dma((NZ, 2, 2)),
            dma((NZ, 6)), dma((NZ, 6)),
            dma((4,)), dma((4,)),
            dma((NZ, 2)), dma((NZ, 2)),
            dma, dma,
            dma, dma,
            dma((NQ,)), dma((NQ,)),
            dma, dma,
            dma((NQ, 2)), dma((NQ, 2)),
            dma((NQ,)), dma((NQ,)),
            pltpu.SemaphoreType.REGULAR,
            pltpu.SemaphoreType.REGULAR,
            pltpu.SemaphoreType.REGULAR,
        ],
        compiler_params=pltpu.CompilerParams(
            collective_id=0, has_side_effects=True, vmem_limit_bytes=48 * 2**20
        ),
        name="sync_and_project",
    )(
        hbm(activations),
        hbm(local_weights[0]),
        hbm(grad_codes[0].reshape(cut)),
        hbm(block_scales[0].T),
        hbm(block_owner.T),
        hbm(global_weights.reshape(cut)),
        hbm(momentum[0].reshape(cut)),
    )
    proj, og, om = pl.pallas_call(
        hand_over,
        out_shape=(
            jax.ShapeDtypeStruct((tok, width), bf),
            jax.ShapeDtypeStruct(cut, bf),
            jax.ShapeDtypeStruct(cut, bf),
        ),
        in_specs=[vmem] * 2,
        out_specs=[any_space] * 3,
        scratch_shapes=[dma((1 + 2 * NQ,))],
        compiler_params=pltpu.CompilerParams(vmem_limit_bytes=16 * 2**20),
        name="hand_over",
    )(proj, res)
    return proj, og.reshape(rows, width), om.reshape(rows, width)


def solution(mesh):
    return jax.shard_map(
        body,
        mesh=mesh,
        in_specs=(
            P(("island", "fsdp"), None),
            P("island", "fsdp", None),
            P("island", "fsdp", None),
            P("island", "fsdp", None),
            P("fsdp", None),
            P("island", "fsdp", None),
            P("fsdp", None),
        ),
        out_specs=(P(("island", "fsdp"), None), P("fsdp", None), P("fsdp", None)),
        check_vma=False,
    )
```

```python
import functools

import jax
import jax.numpy as jnp
from jax import lax
from jax.experimental import pallas as pl
from jax.experimental.pallas import tpu as pltpu
from jax.sharding import PartitionSpec as P

MESH = pl.DeviceIdType.MESH

outer_momentum = 0.9
outer_rate = 0.7

NX, NZ, NY = 4, 4, 8
NQ = 4
Q = 32
QF = 1 if Q < 32 else 2


def gather_kernel(
    act, wown, codes, scales, owner, gw, mom,
    proj, res,
    X, W, acc, pacc,
    cbuf, stg, rbuf, scbuf, rsc, owbuf, gbuf, tmp, tmpt, zs, zm, zrs, zrm,
    lsem, zsem_s, zsem_r, xsem_s, xsem_r, qxs, qxr, qzs, qzr,
    acts, actr, pts, ptr_, rss, rsr, scs, scr, zhs, zhr, ags, agr, farsem, heresem, upsem,
):
    i, f = lax.axis_index("island"), lax.axis_index("fsdp")
    zh, y = i // NY, i % NY
    z, x, c = f // (2 * NX), (f // 2) % NX, f % 2
    rows = wown.shape[0]
    p = rows - Q
    cut = p // 32 * 16
    tok = act.shape[0]
    depth = rows

    def fs(zz, xx, cc):
        return {"fsdp": zz * 2 * NX + xx * 2 + cc}

    def isl(hh, yy):
        return {"island": hh * NY + yy}

    xl, xr, xo = (x + NX - 1) % NX, (x + 1) % NX, (x + 2) % NX
    right, left = fs(z, xr, c), fs(z, xl, c)
    partner = fs(z, x, 1 - c)
    far = isl(1 - zh, y)

    def rcopy(src, dst, ss, rs, dev):
        return pltpu.make_async_remote_copy(
            src_ref=src, dst_ref=dst, send_sem=ss, recv_sem=rs, device_id=dev, device_id_type=MESH
        )

    g = y // 5
    rank = (1 - g) * (2 * y - 1 + (NY - y) // NY) + g * 2 * (NY - y)

    def rank_of(t):
        gt = t // 5
        return (1 - gt) * (2 * t - 1 + (NY - t) // NY) + gt * 2 * (NY - t)

    up, down = fs(z + 1, x, c), fs(z - 1, x, c)
    bar = pltpu.get_barrier_semaphore()

    def hello(dev):
        pl.semaphore_signal(bar, inc=1, device_id=dev, device_id_type=MESH)

    ld_w = pltpu.make_async_copy(wown, W.at[z * NX + x], lsem.at[1])
    ld_w.start()
    for dev in (right, left, partner):
        hello(dev)

    @pl.when(z < NZ - 1)
    def _():
        hello(up)

    for d in range(1, NY):
        t = (y + d) % NY

        @pl.when(rank_of(t) > rank)
        def _():
            hello(isl(zh, t))

    @pl.when(zh == 0)
    def _():
        hello(far)

    kown = z * NX + x
    ld_codes = pltpu.make_async_copy(codes, cbuf, lsem.at[0])
    ld_codes.start()
    hw = mom.shape[3] // 2
    ld_mom = [
        pltpu.make_async_copy(
            mom.at[:, :, :, pl.ds(ch * hw, hw)], stg.at[:, :, ch, pl.ds(16, 16), :], lsem.at[(2, 7)[ch]]
        )
        for ch in range(2)
    ]
    for ld in ld_mom:
        ld.start()
    ld_sc = pltpu.make_async_copy(scales, scbuf, lsem.at[3])
    ld_sc.start()
    ld_ow = pltpu.make_async_copy(owner, owbuf, lsem.at[4])
    ld_ow.start()
    ld_gw = pltpu.make_async_copy(gw.at[y], gbuf, lsem.at[5])
    ld_gw.start()

    below = (z + NZ - 1) // NZ
    ld_w.wait()
    pl.semaphore_wait(bar, 3 + below + rank + zh)

    def zanswer():
        @pl.when(z > 0)
        def _():
            pl.semaphore_signal(upsem, inc=1, device_id=down, device_id_type=MESH)

    def answer():
        for d in range(1, NY):
            t = (y + d) % NY

            @pl.when(rank_of(t) < rank)
            def _():
                pl.semaphore_signal(heresem, inc=1, device_id=isl(zh, t), device_id_type=MESH)

        @pl.when(zh == 1)
        def _():
            pl.semaphore_signal(farsem, inc=1, device_id=far, device_id_type=MESH)

    def x_start():
        @pl.loop(0, NX * NZ)
        def _(k):
            col = pl.multiple_of((2 * k + c) * depth, depth)
            pltpu.make_async_copy(
                act.at[:, pl.ds(col, depth)], X.at[k, pl.ds(0, tok), :], lsem.at[6]
            ).start()

    def codes_ready():
        ld_codes.wait()

        @pl.loop(0, NY)
        def _(t):
            for ch in range(2):
                code = cbuf[t, :, :, pl.ds(ch * hw, hw)]
                stg[t, :, ch, pl.ds(0, 16), :] = code.astype(jnp.float32).astype(jnp.bfloat16)

        for ld in ld_mom:
            ld.wait()
        ld_sc.wait()

    def peers_here():
        @pl.when(rank < NY - 1)
        def _():
            pl.semaphore_wait(heresem, NY - 1 - rank)

    def half(k, h, at=cut):
        return W.at[k, pl.ds(h * at, at + h * (p - 2 * at)), :]

    def xhalf(j, k, h):
        return half(k, h, cut if j < NZ // 2 else p - cut)

    def qpart(k):
        return W.at[k, pl.ds(p, Q), :]

    def qhalf(k, h):
        return W.at[k, pl.ds(p + h * (Q // QF), Q // QF), :]

    def qrow(r):
        return W.at[pl.ds(r * NX, NX), pl.ds(p, Q), :]

    m = z // 2
    e = z * (1 - m) + (NZ - 1 - z) * m

    def order(j):
        g = j if j >= 2 else j * (1 - e) + (1 - j) * e
        return g * (1 - m) + (NZ - 1 - g) * m

    def xcopy(j, n):
        r = order(j) * NX
        k, h, dev = [
            (r + x, 0, right), (r + x, 1, right), (r + x, 1, left), (r + x, 0, left),
            (r + xl, 0, right), (r + xr, 1, left),
        ][n]
        return rcopy(xhalf(j, k, h), xhalf(j, k, h), xsem_s.at[j, n], xsem_r.at[j, n], dev)

    def xlanded(j, n):
        r = order(j) * NX
        k, h = [(r + xl, 0), (r + xl, 1), (r + xr, 1), (r + xr, 0), (r + xo, 0), (r + xo, 1)][n]
        return rcopy(xhalf(j, k, h), xhalf(j, k, h), xsem_s.at[j, n], xsem_r.at[j, n], right)

    def qxcopy(n):
        k = [kown, kown, z * NX + xl, z * NX + xr][n]
        dev = [right, left, right, left][n]
        ref = qpart(k) if n < 2 else qhalf(k, n - 2)
        return rcopy(ref, ref, qxs.at[n], qxr.at[n], dev)

    def qxlanded(n):
        k = z * NX + [xl, xr, xo, xo][n]
        ref = qpart(k) if n < 2 else qhalf(k, n - 2)
        return rcopy(ref, ref, qxs.at[n], qxr.at[n], right)

    def zcopy(s, h, d):
        k = (z - s if d == 0 else z + s) * NX + x
        return rcopy(half(k, h), half(k, h), zsem_s.at[s, h, d], zsem_r.at[s, h, d], up if d == 0 else down)

    def zlanded(s, h, d):
        k = (z - s if d == 0 else z + s) * NX + x
        return rcopy(half(k, h), half(k, h), zsem_s.at[s - 1, h, d], zsem_r.at[s - 1, h, d], up if d == 0 else down)

    def qzcopy(s, d):
        ref = qrow(z - s if d == 0 else z + s)
        return rcopy(ref, ref, qzs.at[s, d], qzr.at[s, d], up if d == 0 else down)

    def qzlanded(s, d):
        ref = qrow(z - s if d == 0 else z + s)
        return rcopy(ref, ref, qzs.at[s - 1, d], qzr.at[s - 1, d], up if d == 0 else down)

    def has(s, d):
        return z - s >= 0 if d == 0 else z + s <= NZ - 1

    def goes(d):
        return z < NZ - 1 if d == 0 else z > 0

    def zpass(s):
        for h in range(2):
            for d in range(2):
                @pl.when(has(s, d))
                def _():
                    zlanded(s, h, d).wait_recv()

                    @pl.when(goes(d))
                    def _():
                        zcopy(s, h, d).start()

    def qzpass(s):
        for d in range(2):
            @pl.when(has(s, d))
            def _():
                qzlanded(s, d).wait_recv()

                @pl.when(goes(d))
                def _():
                    qzcopy(s, d).start()

    def xsend(j):
        for n in (0, 2, 1, 3):
            xcopy(j, n).start()

    def xpass(j):
        for n in (0, 2):
            xlanded(j, n).wait_recv()
            xcopy(j, 4 + n // 2).start()

    def xdone(j):
        for n in (1, 3, 4, 5):
            xlanded(j, n).wait_recv()

    def multiply(k, first=False):
        part = jnp.dot(X[k], W[k], preferred_element_type=jnp.float32)
        if first:
            acc[...] = part
        else:
            acc[...] += part

    def multiply_row(j):
        r = order(j) * NX

        @pl.loop(0, NX)
        def _(n):
            multiply(r + n)

    def last_row():
        r = order(NZ - 1) * NX
        multiply(r + x)
        for n in (1, 3):
            xlanded(NZ - 1, n).wait_recv()
        multiply(r + xl)
        multiply(r + xr)
        for n in (4, 5):
            xlanded(NZ - 1, n).wait_recv()
        for h in range(2):
            cols = pl.ds(h * hw, hw)
            acc[pl.ds(tok, tok), cols] += jnp.dot(
                X[r + xo, pl.ds(tok, tok), :], W[r + xo, :, cols], preferred_element_type=jnp.float32
            )
            pcopy(h).start()

    def last_own():
        r = order(NZ - 1) * NX
        acc[pl.ds(0, tok), :] += jnp.dot(
            X[r + xo, pl.ds(0, tok), :], W[r + xo], preferred_element_type=jnp.float32
        )

    def rs_copy(q, d):
        t = (y + d) % NY
        return rcopy(stg.at[t, q // 2, q % 2], rbuf.at[q, d - 1], rss.at[q], rsr.at[q], isl(zh, t))

    def sc_copy(d):
        t = (y + d) % NY
        lanes = pl.ds(pl.multiple_of((t // 4) * 128, 128), 128)
        return rcopy(scbuf.at[:, lanes], rsc.at[d - 1], scs, scr, isl(zh, t))

    def zh_copies(q):
        return (
            rcopy(zs.at[q], zrs.at[q], zhs.at[q, 0], zhr.at[q, 0], far),
            rcopy(zm.at[q], zrm.at[q], zhs.at[q, 1], zhr.at[q, 1], far),
        )

    def ag_copy(q, d):
        return rcopy(res.at[q, y], res.at[q, y], ags.at[q], agr.at[q], isl(zh, (y + d) % NY))

    far_first = (4, 3, 5, 2, 6, 1, 7)

    def small_columns():
        rcopy(rsc, rsc, scs, scr, far).wait_recv()
        ld_ow.wait()
        lanes = pl.ds(pl.multiple_of((y // 4) * 128, 128), 128)
        tmp[...] = jnp.zeros_like(tmp)
        tmp[pl.ds(0, 4), :] = scbuf[:, lanes]
        for d in range(1, NY):
            tmp[pl.ds(4 * d, 4), :] = rsc[d - 1]
        tmp[pl.ds(32, 4), :] = owbuf[:, lanes].astype(jnp.float32)
        tmpt[...] = tmp[...].T

    def partial(q):
        rcopy(rbuf.at[q], rbuf.at[q], rss.at[q], rsr.at[q], far).wait_recv()
        cols = tmpt[pl.ds(pl.multiple_of(32 * (y % 4) + 16 * (q // 2), 16), 16), :]
        for n in range(2):
            lanes = pl.ds(128 * n, 128)
            b = 2 * (q % 2) + n
            total = jnp.zeros((16, 128), jnp.float32)
            held = jnp.zeros((16, 128), jnp.float32)
            own = jnp.broadcast_to(cols[:, 32 + b : 33 + b], (16, 128))
            for d in range(NY):
                if d == 0:
                    code, state = (
                        stg[y, q // 2, q % 2, pl.ds(0, 16), lanes],
                        stg[y, q // 2, q % 2, pl.ds(16, 16), lanes],
                    )
                else:
                    code, state = (
                        rbuf[q, d - 1, pl.ds(0, 16), lanes],
                        rbuf[q, d - 1, pl.ds(16, 16), lanes],
                    )
                total += code.astype(jnp.float32) * cols[:, 4 * d + b : 4 * d + b + 1]
                who = (zh * NY + (y + NY - d) % NY).astype(jnp.float32)
                held += jnp.where(own == who, state.astype(jnp.float32), 0.0)
            zs[q, :, lanes] = total
            zm[q, :, lanes] = held.astype(jnp.bfloat16)
        for cp in zh_copies(q):
            cp.start()

    def finish(q):
        for cp in zh_copies(q):
            cp.wait_recv()
        mean = (zs[q] + zrs[q]) * (1.0 / (2 * NY))
        held = zm[q].astype(jnp.float32) + zrm[q].astype(jnp.float32)
        fresh = outer_momentum * held + mean
        old = gbuf[q // 2, :, pl.ds((q % 2) * hw, hw)].astype(jnp.float32)
        updated = old - outer_rate * (mean + outer_momentum * fresh)
        res[q, y, 0] = updated.astype(jnp.bfloat16)
        res[q, y, 1] = fresh.astype(jnp.bfloat16)
        for d in far_first:
            ag_copy(q, d).start()

    def zstart(d):
        @pl.when(goes(d))
        def _():
            if d == 0:
                pl.semaphore_wait(upsem, 1)
            for h in range(2):
                zcopy(0, h, d).start()

    def qzstart():
        for d in range(2):
            @pl.when(goes(d))
            def _():
                qzcopy(0, d).start()

    def rs_start(q):
        if q == 0:
            for d in far_first:
                sc_copy(d).start()
        for d in far_first:
            rs_copy(q, d).start()

    def act_start():
        @pl.loop(0, NX * NZ)
        def _(k):
            col = pl.multiple_of((2 * k + 1 - c) * depth, depth)
            rcopy(act.at[:, pl.ds(col, depth)], X.at[k, pl.ds(tok, tok), :], acts, actr, partner).start()

    act_in = rcopy(X.at[:, pl.ds(tok, tok), :], X.at[:, pl.ds(tok, tok), :], acts, actr, partner)

    def act_wait():
        act_in.wait_recv()
        pltpu.make_async_copy(X.at[:, pl.ds(0, tok), :], X.at[:, pl.ds(0, tok), :], lsem.at[6]).wait()

    def qstart():
        qxcopy(0).start()
        qxcopy(1).start()

    def qpass():
        for n in range(2):
            qxlanded(n).wait_recv()
            if n < QF:
                qxcopy(2 + n).start()

    def qdone():
        for n in range(QF):
            qxlanded(2 + n).wait_recv()

    def far_here():
        pl.semaphore_wait(farsem, 1)

    def pcopy(h):
        cols = pl.ds(h * hw, hw)
        return rcopy(acc.at[pl.ds(tok, tok), cols], pacc.at[:, cols], pts.at[h], ptr_.at[h], partner)

    res_in = [
        rcopy(res.at[q, pl.ds(0, 7)], res.at[q, pl.ds(0, 7)], ags.at[q], agr.at[q], far)
        for q in range(NQ)
    ]

    def gathered(q):
        res_in[q].wait_recv()

    def finish_proj():
        for h in range(2):
            cols = pl.ds(h * hw, hw)
            pcopy(h).wait()
            proj[:, cols] = (acc[pl.ds(0, tok), cols] + pacc[:, cols]).astype(jnp.bfloat16)

    def sent_a():
        for j in range(NZ):
            for n in range(6):
                xcopy(j, n).wait_send()
        for n in range(2 + QF):
            qxcopy(n).wait_send()
        for s in range(NZ - 1):
            for d in range(2):
                @pl.when(has(s, d) & goes(d))
                def _():
                    for h in range(2):
                        zcopy(s, h, d).wait_send()
                    qzcopy(s, d).wait_send()
        act_in.wait_send()

    def sent_b():
        rcopy(rsc, rsc, scs, scr, far).wait_send()
        for q in range(NQ):
            rcopy(rbuf.at[q], rbuf.at[q], rss.at[q], rsr.at[q], far).wait_send()
            for cp in zh_copies(q):
                cp.wait_send()
            res_in[q].wait_send()

    qstart()
    xsend(0)
    zanswer()
    zstart(1)
    answer()
    codes_ready()
    act_start()
    x_start()
    zstart(0)
    @pl.when(zh == 1)
    def _():
        peers_here()

    @pl.when(zh == 1)
    def _():
        rs_start(0)
        rs_start(1)
        rs_start(2)
        rs_start(3)

    qpass()
    @pl.when(zh == 0)
    def _():
        peers_here()

    @pl.when(zh == 0)
    def _():
        rs_start(0)
        rs_start(1)
        rs_start(2)
        rs_start(3)

    zpass(1)
    xsend(1)
    xpass(0)
    qdone()
    qzstart()
    @pl.when(zh == 1)
    def _():
        small_columns()
        partial(0)
        partial(1)
        partial(2)

    zpass(2)
    xsend(2)
    @pl.when(zh == 1)
    def _():
        partial(3)

    xpass(1)
    qzpass(1)
    @pl.when(zh == 0)
    def _():
        far_here()

    @pl.when(zh == 0)
    def _():
        small_columns()
        partial(0)
        partial(1)
        partial(2)

    xdone(0)
    act_wait()
    acc[...] = jnp.zeros_like(acc)
    multiply_row(0)
    ld_gw.wait()
    finish(0)
    @pl.when(zh == 0)
    def _():
        partial(3)

    zpass(3)
    xsend(3)
    xpass(2)
    qzpass(2)
    finish(1)
    xdone(1)
    multiply_row(1)
    finish(2)
    xpass(3)
    finish(3)
    xdone(2)
    multiply_row(2)
    qzpass(3)
    last_row()
    last_own()
    for q in range(NQ):
        gathered(q)
    sent_a()
    sent_b()
    finish_proj()


def hand_over(proj, res, out, og, om, sem):
    hw = res.shape[4]
    copies = [pltpu.make_async_copy(proj, out, sem.at[0])]
    for n, held in enumerate((og, om)):
        for q in range(NQ):
            part = held.at[:, q // 2, :, pl.ds(q % 2 * hw, hw)]
            copies.append(pltpu.make_async_copy(res.at[q, :, n], part, sem.at[1 + NQ * n + q]))
    for cp in copies:
        cp.start()
    for cp in copies:
        cp.wait()


def body(
    activations, local_weights, grad_codes, block_scales, global_weights, momentum, block_owner
):
    tok, model = activations.shape
    rows, width = local_weights.shape[1:]
    nk = NX * NZ
    cut = (NY, 2, rows // (2 * NY), width)
    any_space = pl.BlockSpec(memory_space=pl.ANY)
    vmem = pl.BlockSpec(memory_space=pltpu.VMEM)
    hbm = functools.partial(pltpu.with_memory_space_constraint, memory_space=pltpu.HBM)
    bf, f32 = jnp.bfloat16, jnp.float32
    dma = pltpu.SemaphoreType.DMA
    proj, res = pl.pallas_call(
        gather_kernel,
        out_shape=(
            pltpu.VMEM((tok, width), bf),
            pltpu.VMEM((NQ, NY, 2, 16, width // 2), bf),
        ),
        in_specs=[any_space] * 7,
        out_specs=(vmem, vmem),
        scratch_shapes=[
            pltpu.VMEM((nk, 2 * tok, rows), bf),
            pltpu.VMEM((nk, rows, width), bf),
            pltpu.VMEM((2 * tok, width), f32),
            pltpu.VMEM((tok, width), f32),
            pltpu.VMEM(cut, jnp.int32),
            pltpu.VMEM((NY, 2, 2, 32, width // 2), bf),
            pltpu.VMEM((NQ, NY - 1, 32, width // 2), bf),
            pltpu.VMEM((4, rows), f32),
            pltpu.VMEM((NY - 1, 4, 128), f32),
            pltpu.VMEM((4, rows), jnp.int32),
            pltpu.VMEM((2, 16, width), bf),
            pltpu.VMEM((128, 128), f32),
            pltpu.VMEM((128, 128), f32),
            pltpu.VMEM((NQ, 16, width // 2), f32),
            pltpu.VMEM((NQ, 16, width // 2), bf),
            pltpu.VMEM((NQ, 16, width // 2), f32),
            pltpu.VMEM((NQ, 16, width // 2), bf),
            dma((8,)),
            dma((NZ, 2, 2)), dma((NZ, 2, 2)),
            dma((NZ, 6)), dma((NZ, 6)),
            dma((4,)), dma((4,)),
            dma((NZ, 2)), dma((NZ, 2)),
            dma, dma,
            dma((2,)), dma((2,)),
            dma((NQ,)), dma((NQ,)),
            dma, dma,
            dma((NQ, 2)), dma((NQ, 2)),
            dma((NQ,)), dma((NQ,)),
            pltpu.SemaphoreType.REGULAR,
            pltpu.SemaphoreType.REGULAR,
            pltpu.SemaphoreType.REGULAR,
        ],
        compiler_params=pltpu.CompilerParams(
            collective_id=0, has_side_effects=True, vmem_limit_bytes=48 * 2**20
        ),
        name="sync_and_project",
    )(
        hbm(activations),
        hbm(local_weights[0]),
        hbm(grad_codes[0].reshape(cut)),
        hbm(block_scales[0].T),
        hbm(block_owner.T),
        hbm(global_weights.reshape(cut)),
        hbm(momentum[0].reshape(cut)),
    )
    proj, og, om = pl.pallas_call(
        hand_over,
        out_shape=(
            jax.ShapeDtypeStruct((tok, width), bf),
            jax.ShapeDtypeStruct(cut, bf),
            jax.ShapeDtypeStruct(cut, bf),
        ),
        in_specs=[vmem] * 2,
        out_specs=[any_space] * 3,
        scratch_shapes=[dma((1 + 2 * NQ,))],
        compiler_params=pltpu.CompilerParams(vmem_limit_bytes=16 * 2**20),
        name="hand_over",
    )(proj, res)
    return proj, og.reshape(rows, width), om.reshape(rows, width)


def solution(mesh):
    return jax.shard_map(
        body,
        mesh=mesh,
        in_specs=(
            P(("island", "fsdp"), None),
            P("island", "fsdp", None),
            P("island", "fsdp", None),
            P("island", "fsdp", None),
            P("fsdp", None),
            P("island", "fsdp", None),
            P("fsdp", None),
        ),
        out_specs=(P(("island", "fsdp"), None), P("fsdp", None), P("fsdp", None)),
        check_vma=False,
    )
```
